256 devices in a mesh: seg: 64 (over x, z, core), det: 4 (over y).
Axes of the slice: x: 4, y: 4, z: 8, core: 2. Of those that a mesh axis runs over, the one named last changes fastest.
Arguments:
- strain: float32 [4, 64, 4096], P('det', 'seg'), may hold values from -6 to 6
- antenna: float32 [2, 4], replicated, may hold values from -1 to 1
- delays: int32 [4], replicated, may hold values from -24 to 24
- template_bank: bfloat16 [64, 256, 4096], P('seg', 'det'), may hold values from -6 to 6
- duration_bin: int32 [64, 256], P('seg', 'det'), may hold values from 0 to 7
- owner_seg: int32 [64, 2048, 1], P('seg', 'det'), may hold values from 0 to 63; in each aligned block of 512 rows (0 to 511, 512 to 1023, ..., all dimensions but the last counted through in order) at most 16 rows name the same one
- slot_index: int32 [64, 2048], P('seg', 'det'), may hold values from 0 to 63
Outputs:
- snr_squared: float32 [64, 2048, 1024], P('seg', 'det')
The draws below stay inside these ranges and needn't reach their ends.
Inputs may be any that keep to these rules, and one draw needn't show every extreme that they name: `owner_seg`: in each device's rows of 512 requests no owner is named more than 16 times, a bound that some block reaches.
All inputs are finite; a program needn't handle non-finite values.
Results may differ from the reference program's by a relative error of at most 0.0031.
Values may be sent and summed in bfloat16 or wider, within the bound.
No kernel may reach another device: no remote copies, remote signals or barrier semaphores. Data moves between devices by JAX's collectives and lax.ppermute only.
A program may use at most 128 MiB of HBM per device.

```python
import math
import jax
import jax.numpy as jnp
import numpy as np
from jax import lax

F = 2048
STEP = 1024
DETS = 4
NBINS = 8
MAXLAG = 24
REQ_DEV = 512
TPD = 64
SEGS = 64
REQS = 2048
CAP = 16
N_SEG = 64
N_DET = 4


def place_ends(values, stream_key, low, high):
    index_at = [jax.random.randint(jax.random.fold_in(stream_key, axis), (), 0, length) for axis, length in enumerate(values.shape)]
    widest = values.shape.index(max(values.shape))
    neighbour = index_at[:widest] + [(index_at[widest] + 1) % values.shape[widest]] + index_at[widest + 1:]
    return values.at[tuple(index_at)].set(low).at[tuple(neighbour)].set(high)


def levels(stream_key, extent, pieces, low, high):
    def one(dim, parts):
        draws = jax.random.uniform(jax.random.fold_in(jax.random.fold_in(stream_key, 6), dim), (parts,), jnp.float32, low / len(pieces), high / len(pieces))
        return jnp.repeat(jnp.exp(draws), extent[dim] // parts).reshape((-1,) + (1,) * (len(extent) - dim - 1))

    loudness = one(*pieces[0])
    for cut in pieces[1:]:
        loudness = loudness * one(*cut)
    return loudness


def assign_block(own_key, own, number, rows, count, top, most, skew):
    ranking = jax.random.permutation(own_key, count)
    crowded, usual = shares(count, rows * top, most, skew, True), shares(count, rows * top, most, skew, False)
    places = jnp.arange(count)

    def named(lengths, offset_by):
        used = int((lengths > 0).sum())
        fixed = max(1, used // 4)
        moved = fixed + (places - fixed + offset_by * (used - fixed)) % max(1, count - fixed)
        return jnp.zeros((count,), jnp.int32).at[ranking[jnp.where(places < fixed, places, moved)]].set(jnp.asarray(lengths, jnp.int32))

    lengths = jnp.where(number % 4 == 0, named(crowded, number // 4), named(usual, number - number // 4 - 1))
    mixed = jax.random.permutation(jax.random.fold_in(own, 3), count)
    donor, taker = mixed[0:count // 2 * 2:2], mixed[1:count // 2 * 2:2]
    margin = jnp.minimum(lengths[donor] - 1, most - lengths[taker]) // 2
    margin = jnp.where((donor == ranking[0]) | (taker == ranking[0]) | (lengths[taker] == 0), 0, jnp.maximum(margin, 0))
    moved = jax.random.randint(jax.random.fold_in(own, 4), (count // 2,), 0, 1 << 20) % (margin + 1)
    lengths = lengths.at[donor].add(-moved).at[taker].add(moved)
    members = jnp.searchsorted(jnp.cumsum(lengths), jnp.arange(rows * top), side="right").astype(jnp.int32)
    table = members.reshape(top, rows).T
    table = table[jax.random.permutation(jax.random.fold_in(own, 1), rows)]
    offset_by = jax.random.randint(jax.random.fold_in(own, 2), (rows, 1), 0, top)
    return jnp.take_along_axis(table, (jnp.arange(top)[None, :] + offset_by) % top, axis=1)


def shares(amount, total, most, skew, full):
    portions = [(1 << 20) // math.isqrt(rank ** skew) + 1 for rank in range(1, amount + 1)]
    largest = most if full else min(most, max(-(-total // amount), total * portions[0] // sum(portions)))
    least = 1 if total - largest >= amount - 1 else 0
    holding, spare = [largest] + [least] * (amount - 1), total - largest - least * (amount - 1)
    while spare > 0:
        candidates = [i for i in range(1, amount) if holding[i] < largest] or [i for i in range(1, amount) if holding[i] < most]
        mass, remaining = sum([portions[i] for i in candidates]), spare
        for i in candidates:
            more = min(most - holding[i], max(1, remaining * portions[i] // mass), spare)
            holding[i] = holding[i] + more
            spare = spare - more
    return np.array(holding)


def gaussian(own_key, shape, width, limit, shards=(), held_as=jnp.bfloat16):
    level = levels(own_key, shape, shards, -0.22, 0.18) if shards else 1.0
    array = jax.random.normal(own_key, shape, jnp.float32) * width * level
    return jnp.minimum(jnp.maximum(array, -limit), limit).astype(held_as)


def setup_inputs(seed: int = 0) -> dict:
    seeds = jax.random.split(jax.random.key(seed), 8)
    strain = gaussian(seeds[0], (DETS, SEGS, 2 * F), 1.0, 6.0, ((0, 4), (1, 64)), jnp.float32)
    antenna = jnp.clip(jax.random.uniform(seeds[1], (2, DETS), jnp.float32, -1.0, 1.0), -1.0, 1.0)
    delays = place_ends(jax.random.randint(seeds[2], (DETS,), -MAXLAG, MAXLAG + 1), jax.random.fold_in(seeds[2], 1), -MAXLAG, MAXLAG).astype(jnp.int32)
    template_bank = gaussian(seeds[3], (SEGS, N_DET * TPD, 2 * F), 1.0, 6.0, ((0, 64), (1, 4)))
    duration_bin = place_ends(jax.random.randint(seeds[4], (SEGS, N_DET * TPD), 0, NBINS), jax.random.fold_in(seeds[4], 1), 0, NBINS - 1).astype(jnp.int32)
    owner_seg_keys = jax.random.split(jax.random.fold_in(seeds[5], 1), SEGS * REQS // REQ_DEV)
    owner_seg_turns = jax.random.permutation(jax.random.fold_in(seeds[5], 3), SEGS * REQS // REQ_DEV)
    owner_seg = jax.vmap(lambda own, number: assign_block(jax.random.fold_in(seeds[5], 2), own, number, REQ_DEV, N_SEG, 1, CAP, 2))(owner_seg_keys, owner_seg_turns).reshape((SEGS, REQS, 1))
    slot_index = place_ends(jax.random.randint(seeds[6], (SEGS, REQS), 0, TPD), jax.random.fold_in(seeds[6], 1), 0, TPD - 1).astype(jnp.int32)
    return {"strain": strain, "antenna": antenna, "delays": delays, "template_bank": template_bank, "duration_bin": duration_bin, "owner_seg": owner_seg, "slot_index": slot_index}


def lag_basis(half_width, lag_count):
    bin_index = jnp.arange(half_width, dtype=jnp.int32)[:, None]
    lag_index = jnp.arange(lag_count, dtype=jnp.int32)[None, :]
    phases = ((bin_index * lag_index) % (2 * half_width)).astype(jnp.float32) * (math.pi / half_width)
    cosines = jnp.cos(phases)
    sine_part = jnp.sin(phases)
    upper_half = jnp.concatenate([cosines, sine_part], 1)
    lower_half = jnp.concatenate([-sine_part, cosines], 1)
    return jnp.concatenate([upper_half, lower_half], 0).astype(jnp.bfloat16)


def shifted(strain_rows, delays):
    half_width = strain_rows.shape[-1] // 2
    bin_index = jnp.arange(half_width, dtype=jnp.int32)
    phases = ((bin_index[None, :] * delays[:, None]) % (2 * half_width)).astype(jnp.float32) * (-math.pi / half_width)
    real_part = strain_rows[:, :half_width]
    imag_part = strain_rows[:, half_width:]
    cos_rot = jnp.cos(phases)
    sin_rot = jnp.sin(phases)
    return jnp.concatenate([real_part * cos_rot - imag_part * sin_rot, real_part * sin_rot + imag_part * cos_rot], 1)


def combine(antenna, shifted_rows):
    return jnp.sum(antenna[:, :, None] * shifted_rows[None], axis=1)


def masked_bank(template_bank, duration_bin):
    half_width = template_bank.shape[-1] // 2
    first_bin = duration_bin * (half_width // (2 * NBINS))
    bin_index = jnp.arange(2 * half_width, dtype=jnp.int32) % half_width
    kept_bins = bin_index >= first_bin[..., None]
    return jnp.where(kept_bins, template_bank, jnp.zeros_like(template_bank))


def template_norm(masked):
    widened = masked.astype(jnp.float32)
    return jnp.sum(widened * widened, -1)


def correlate(network, masked, norm_sq, basis):
    half_width = masked.shape[-1] // 2
    lag_count = basis.shape[1] // 2
    widened = masked.astype(jnp.float32)[:, None]
    net_real = network[:, :, None, :half_width]
    net_imag = network[:, :, None, half_width:]
    tmpl_real = widened[..., :half_width]
    tmpl_imag = widened[..., half_width:]
    prod_real = net_real * tmpl_real + net_imag * tmpl_imag
    prod_imag = net_imag * tmpl_real - net_real * tmpl_imag
    spectra = jnp.concatenate([prod_real, prod_imag], -1).astype(jnp.bfloat16)
    shape_out = spectra.shape[:-1]
    lagged = jnp.dot(spectra.reshape(-1, 2 * half_width), basis, preferred_element_type=jnp.float32)
    lagged = lagged.reshape(shape_out + (2 * lag_count,))
    squares = jnp.sum(lagged * lagged, 1)
    return (squares[..., :lag_count] + squares[..., lag_count:]) / norm_sq[..., None]


def reference(strain, antenna, delays, template_bank, duration_bin, owner_seg, slot_index):
    masked = masked_bank(template_bank, duration_bin)
    basis = lag_basis(F, STEP)
    row_detector = jnp.arange(REQS, dtype=jnp.int32) // REQ_DEV

    def per_segment(packed):
        strain_rows, owners_row, slots_row = packed
        network = combine(antenna, shifted(strain_rows, delays))
        bank_index = row_detector * TPD + slots_row
        picked = masked[owners_row, bank_index]
        return correlate(network[None], picked[None], template_norm(picked)[None], basis)[0]

    return lax.map(per_segment, (jnp.transpose(strain, (1, 0, 2)), owner_seg[:, :, 0], slot_index))
```

```python
import functools
import math

import jax
import jax.numpy as jnp
import numpy as np
from jax import lax
from jax.experimental import pallas as pl
from jax.experimental.pallas import tpu as pltpu
from jax.sharding import PartitionSpec as P

HALF = 2048
WIDE = 2 * HALF
STEP = 1024
NX, NZ, NC = 4, 8, 2
PEERS = NX * NC
CAP = 16
SLOTS = 64
CLASSES = 16
T1 = 256
QS = 4
BIG = 3.0e38

LANE = np.arange(128)
FREQ = 128 * (LANE % 16)[None, :] + 16 * (LANE // 16)[None, :] + np.arange(CLASSES)[:, None]


def class_basis():
    t = np.arange(T1)
    ang = ((FREQ[:, :, None] * t[None, None, :]) % WIDE) * (math.pi / HALF)
    c, s = np.cos(ang), np.sin(ang)
    upper = np.concatenate([c, s], 2)
    lower = np.concatenate([-s, c], 2)
    return np.concatenate([upper, lower], 1).astype(np.float32).astype(jnp.bfloat16)


def bank_kernel(bank_ref, dur_ref, out_ref):
    lane = lax.broadcasted_iota(jnp.int32, (16, 128), 1)

    def rows(i, _):
        r = pl.ds(pl.multiple_of(i * 16, 16), 16)
        dur = dur_ref[r, :]
        for c in range(2):
            x = []
            for g in range(16):
                v = bank_ref[r, c * HALF + g * 128 : c * HALF + (g + 1) * 128].astype(jnp.float32)
                x.append(jnp.where(dur <= g, v, 0.0))
            for k in range(4):
                b = 1 << k
                up = (lane & b) != 0
                for g in range(16):
                    if g & b:
                        continue
                    lo, hi = x[g], x[g | b]
                    x[g] = jnp.where(up, pltpu.roll(hi, b, 1), lo)
                    x[g | b] = jnp.where(up, hi, pltpu.roll(lo, 128 - b, 1))
            for f2 in range(16):
                at = f2 * 256 + c * 128
                out_ref[r, at : at + 128] = x[f2].astype(jnp.bfloat16)
        return 0

    lax.fori_loop(0, 4, rows, 0)


def prepare_bank(bank, dur):
    return pl.pallas_call(
        bank_kernel,
        out_shape=jax.ShapeDtypeStruct((SLOTS, WIDE), jnp.bfloat16),
        in_specs=[pl.BlockSpec(memory_space=pltpu.VMEM)] * 2,
        out_specs=pl.BlockSpec(memory_space=pltpu.VMEM),
        compiler_params=pltpu.CompilerParams(vmem_limit_bytes=16 << 20),
        cost_estimate=pl.CostEstimate(flops=4 << 20, bytes_accessed=1 << 20, transcendentals=0),
        name="prepare_bank",
    )(bank, dur)


def rotate(re, im, k):
    k %= 16
    if k == 0:
        return re, im
    if k == 4:
        return -im, re
    if k == 8:
        return -re, -im
    if k == 12:
        return im, -re
    c, s = math.cos(math.pi * k / 8), math.sin(math.pi * k / 8)
    return re * c - im * s, re * s + im * c


def filter_kernel(count, *refs):
    banks = refs[:count]
    slots_ref, coh_ref, basis_ref, out_ref, spec, xs, acc = refs[count:]
    lane = lax.broadcasted_iota(jnp.int32, (PEERS * CAP, SLOTS), 1)
    for i in range(count):
        onehot = (slots_ref[i] == lane).astype(jnp.bfloat16)
        nsq = jnp.zeros((PEERS * CAP, 128), jnp.float32)
        for a in range(4):
            for b in range(4):
                f2 = a + 4 * b
                at = f2 * 256
                picked = jnp.dot(
                    onehot, banks[i][:, at : at + 256], preferred_element_type=jnp.float32
                )
                tr, ti = picked[:, :128], picked[:, 128:]
                nsq = nsq + (tr * tr + ti * ti)
                for s in range(PEERS):
                    rs = slice(s * CAP, (s + 1) * CAP)
                    trs, tis = tr[rs], ti[rs]
                    for p in range(2):
                        nr = coh_ref[2 * s + p : 2 * s + p + 1, at : at + 128]
                        ni = coh_ref[2 * s + p : 2 * s + p + 1, at + 128 : at + 256]
                        row = p * PEERS * CAP + s * CAP
                        spec[row : row + CAP, 0:128] = (nr * trs + ni * tis).astype(jnp.bfloat16)
                        spec[row : row + CAP, 128:256] = (ni * trs - nr * tis).astype(jnp.bfloat16)
                xs[b] = jnp.dot(spec[...], basis_ref[f2], preferred_element_type=jnp.float32)
            norm = jnp.sum(nsq, axis=1, keepdims=True) if a == 3 else None
            for s in range(PEERS):
                power = [None] * QS
                for p in range(2):
                    row = p * PEERS * CAP + s * CAP
                    rs = slice(row, row + CAP)
                    xr = [xs[b, rs, :T1] for b in range(4)]
                    xi = [xs[b, rs, T1:] for b in range(4)]
                    e0r, e0i, e1r, e1i = xr[0] + xr[2], xi[0] + xi[2], xr[0] - xr[2], xi[0] - xi[2]
                    o0r, o0i, o1r, o1i = xr[1] + xr[3], xi[1] + xi[3], xr[1] - xr[3], xi[1] - xi[3]
                    y = [
                        (e0r + o0r, e0i + o0i),
                        (e1r - o1i, e1i + o1r),
                        (e0r - o0r, e0i - o0i),
                        (e1r + o1i, e1i - o1r),
                    ]
                    for q in range(QS):
                        re, im = rotate(*y[q], a * q)
                        if a > 0:
                            re = re + acc[q, rs, :T1]
                            im = im + acc[q, rs, T1:]
                        if a < 3:
                            acc[q, rs, :T1] = re
                            acc[q, rs, T1:] = im
                        else:
                            w = re * re + im * im
                            power[q] = w if p == 0 else power[q] + w
                if a == 3:
                    n = norm[s * CAP : (s + 1) * CAP]
                    for q in range(QS):
                        v = jnp.where(n > 0.0, jnp.minimum(power[q] / n, BIG), -1.0)
                        out_ref[s, i, :, q * T1 : (q + 1) * T1] = v.astype(jnp.bfloat16)


def filter_banks(banks, slots, coh, basis):
    count = len(banks)
    return pl.pallas_call(
        functools.partial(filter_kernel, count),
        out_shape=jax.ShapeDtypeStruct((PEERS, count, CAP, STEP), jnp.bfloat16),
        in_specs=[pl.BlockSpec(memory_space=pltpu.VMEM)] * (count + 3),
        out_specs=pl.BlockSpec(memory_space=pltpu.VMEM),
        scratch_shapes=[
            pltpu.VMEM((2 * PEERS * CAP, 256), jnp.bfloat16),
            pltpu.VMEM((4, 2 * PEERS * CAP, 2 * T1), jnp.float32),
            pltpu.VMEM((QS, 2 * PEERS * CAP, 2 * T1), jnp.float32),
        ],
        compiler_params=pltpu.CompilerParams(vmem_limit_bytes=32 << 20),
        cost_estimate=pl.CostEstimate(
            flops=count * (3 << 30), bytes_accessed=(5 << 20) + count * (1 << 20), transcendentals=0
        ),
        name=f"filter{count}",
    )(*banks, slots, coh, basis)


def per_device(basis, strain, antenna, delays, template_bank, duration_bin, owner_seg, slot_index):
    seg = lax.axis_index("seg")
    det = lax.axis_index("det")
    my_z = (seg // NC) % NZ

    def at(x, z, c):
        return (x * NZ + z) * NC + c

    places = [(x, z, c) for x in range(NX) for z in range(NZ) for c in range(NC)]
    groups = [[at(x, z, c) for x in range(NX) for c in range(NC)] for z in range(NZ)]
    up = [(at(x, z, c), at(x, (z + 1) % NZ, c)) for x, z, c in places]
    down = [(at(x, z, c), at(x, (z - 1) % NZ, c)) for x, z, c in places]

    with jax.named_scope("bank"):
        own = prepare_bank(template_bank[0], duration_bin[0][:, None])

    with jax.named_scope("ring"):
        held = {0: own}
        for k in (1, 2, 3):
            held[-k] = lax.ppermute(held[1 - k], "seg", up)
            held[k] = lax.ppermute(held[k - 1], "seg", down)
        half = SLOTS // 2
        held[4] = jnp.concatenate(
            [lax.ppermute(held[-3][:half], "seg", up), lax.ppermute(held[3][half:], "seg", down)], 0
        )

    with jax.named_scope("strain"):
        delay = lax.dynamic_index_in_dim(delays, det, 0, False)
        freq = jnp.arange(HALF, dtype=jnp.int32)
        phase = (freq * delay % WIDE).astype(jnp.float32) * (-math.pi / HALF)
        cos_rot, sin_rot = jnp.cos(phase), jnp.sin(phase)
        row = strain[0, 0]
        re, im = row[:HALF], row[HALF:]
        mine = jnp.concatenate([re * cos_rot - im * sin_rot, re * sin_rot + im * cos_rot], 0)
        coherent = 0.0
        for k in range(4):
            other = mine
            if k:
                other = lax.ppermute(mine, "det", [((d + k) % 4, d) for d in range(4)])
            weight = lax.dynamic_index_in_dim(antenna, (det + k) % 4, 1, False)
            coherent = coherent + weight[:, None] * other[None, :]
        coherent = coherent.reshape(2, 2, 16, 8, 16).transpose(0, 4, 1, 3, 2).reshape(2 * WIDE)

    with jax.named_scope("requests"):
        owner = owner_seg[0, :, 0]
        slot = slot_index[0]
        n = owner.shape[0]
        hot = (owner[:, None] == jnp.arange(NX * NZ * NC, dtype=jnp.int32)[None, :])
        idx = jnp.arange(n, dtype=jnp.int32)
        earlier = (idx[:, None] > idx[None, :]).astype(jnp.bfloat16)
        before = jnp.dot(earlier, hot.astype(jnp.bfloat16), preferred_element_type=jnp.float32)
        rank = jnp.sum(jnp.where(hot, before, 0.0), 1).astype(jnp.int32)
        peer = (owner // (NZ * NC)) * NC + owner % NC
        dz = ((owner // NC) % NZ - my_z) % NZ
        pos = (peer * NZ + dz) * CAP + rank
        table = jnp.dot(
            slot.astype(jnp.bfloat16)[None, :],
            (pos[:, None] == jnp.arange(PEERS * NZ * CAP, dtype=jnp.int32)[None, :]).astype(jnp.bfloat16),
            preferred_element_type=jnp.float32,
        ).reshape(PEERS, NZ * CAP)

    with jax.named_scope("exchange"):
        packet = jnp.concatenate([jnp.broadcast_to(coherent[None], (PEERS, 2 * WIDE)), table], 1)
        packet = lax.all_to_all(
            packet, "seg", split_axis=0, concat_axis=0, tiled=True, axis_index_groups=groups
        )
        coh = packet[:, : 2 * WIDE].reshape(PEERS * 2, WIDE)
        slots = packet[:, 2 * WIDE :].astype(jnp.int32).reshape(PEERS, NZ, CAP)
        slots = slots.transpose(1, 0, 2).reshape(NZ, PEERS * CAP, 1)

    out = 0.0
    for part in ((0, -1, 1), (-2, 2), (-3, 3, 4)):
        m = len(part)
        with jax.named_scope("filter"):
            chosen = jnp.concatenate([slots[d % NZ : d % NZ + 1] for d in part], 0)
            rows = filter_banks([held[d] for d in part], chosen, coh, basis)
        with jax.named_scope("back"):
            rows = lax.all_to_all(
                rows.reshape(PEERS, m * CAP, STEP),
                "seg",
                split_axis=0,
                concat_axis=0,
                tiled=True,
                axis_index_groups=groups,
            )
        with jax.named_scope("order"):
            place = jnp.full((n,), -1, jnp.int32)
            for j, d in enumerate(part):
                place = jnp.where(dz == d % NZ, (peer * m + j) * CAP + rank, place)
            pick = place[:, None] == jnp.arange(PEERS * m * CAP, dtype=jnp.int32)[None, :]
            out = out + jnp.dot(
                pick.astype(jnp.bfloat16),
                rows.reshape(PEERS * m * CAP, STEP),
                preferred_element_type=jnp.float32,
            )
    return jnp.where(out < 0.0, jnp.nan, out)[None]


def solution(mesh):
    basis = class_basis()
    in_specs = (
        P("det", "seg", None),
        P(),
        P(),
        P("seg", "det", None),
        P("seg", "det"),
        P("seg", "det", None),
        P("seg", "det"),
    )

    def run(*args):
        return jax.shard_map(
            lambda *a: per_device(jnp.asarray(basis), *a),
            mesh=mesh,
            in_specs=in_specs,
            out_specs=P("seg", "det", None),
            check_vma=False,
        )(*args)

    return run
```

```python
import functools
import math

import jax
import jax.numpy as jnp
import numpy as np
from jax import lax
from jax.experimental import pallas as pl
from jax.experimental.pallas import tpu as pltpu
from jax.sharding import PartitionSpec as P

HALF = 2048
WIDE = 2 * HALF
STEP = 1024
NX, NZ, NC = 4, 8, 2
PEERS = NX * NC
ND = 4
CAP = 16
SLOTS = 64
CLASSES = 16
T1 = 256
QS = 4
BIG = 3.0e38
CALLS = {(0, -1, 1, -2, 2): ((0, -1, 1), (-2, 2)), (-3, 3, 4): ((-3, 3, 4),)}
PARTS = tuple(CALLS)

LANE = np.arange(128)
FREQ = 128 * (LANE % 16)[None, :] + 16 * (LANE // 16)[None, :] + np.arange(CLASSES)[:, None]


def class_basis():
    t = np.arange(T1)
    ang = ((FREQ[:, :, None] * t[None, None, :]) % WIDE) * (math.pi / HALF)
    c, s = np.cos(ang), np.sin(ang)
    upper = np.concatenate([c, s], 2)
    lower = np.concatenate([-s, c], 2)
    return np.concatenate([upper, lower], 1).astype(np.float32).astype(jnp.bfloat16)


def to_classes(x, lane):
    for k in range(4):
        b = 1 << k
        up = (lane & b) != 0
        for g in range(16):
            if g & b:
                continue
            lo, hi = x[g], x[g | b]
            x[g] = jnp.where(up, pltpu.roll(hi, b, 1), lo)
            x[g | b] = jnp.where(up, hi, pltpu.roll(lo, 128 - b, 1))
    return x


def lookup(dz, values):
    out = jnp.zeros_like(dz)
    for d, v in enumerate(values):
        if v:
            out = jnp.where(dz == d, v, out)
    return out


def head_kernel(delays_ref, strain_ref, owner_ref, slot_ref, packet_ref, place_ref):
    det, my_z = lax.axis_index("det"), (lax.axis_index("seg") // NC) % NZ
    owner = owner_ref[...]
    n = owner.shape[1]
    peer = (owner // (NZ * NC)) * NC + (owner & 1)
    dz = ((owner >> 1) - my_z) & (NZ - 1)
    part_of, order_of, first_of = [0] * NZ, [0] * NZ, [0] * NZ
    first = 0
    for g, part in enumerate(PARTS):
        for j, d in enumerate(part):
            part_of[d % NZ], order_of[d % NZ], first_of[d % NZ] = g, j, first
        first += len(part) * CAP
    hot = owner == lax.broadcasted_iota(jnp.int32, (PEERS * NZ, n), 0)
    earlier = lax.broadcasted_iota(jnp.int32, (n, n), 0) < lax.broadcasted_iota(jnp.int32, (n, n), 1)
    before = jnp.dot(
        hot.astype(jnp.float32).astype(jnp.bfloat16),
        earlier.astype(jnp.float32).astype(jnp.bfloat16),
        preferred_element_type=jnp.float32,
    )
    rank = jnp.sum(jnp.where(hot, before, 0.0), axis=0, keepdims=True).astype(jnp.int32)
    start = lookup(dz, first_of)
    rank = rank + CAP * lookup(dz, order_of)
    want = (slot_ref[...] + 1).astype(jnp.float32)
    size = lookup(dz, [len(PARTS[g]) * CAP for g in part_of])
    place = (start * PEERS + peer * size + rank).astype(jnp.float32)
    place_ref[...] = jnp.transpose(jnp.broadcast_to(place, (8, n)))
    wanted = jnp.where(peer == lax.broadcasted_iota(jnp.int32, (PEERS, n), 0), want, 0.0)
    spot = (start + rank) == lax.broadcasted_iota(jnp.int32, (NZ * CAP, n), 0)
    table = (
        lax.dot_general(
            wanted.astype(jnp.bfloat16),
            spot.astype(jnp.float32).astype(jnp.bfloat16),
            (((1,), (1,)), ((), ())),
            preferred_element_type=jnp.float32,
        )
        - 1.0
    )

    delay = delays_ref[det]
    row16 = lax.broadcasted_iota(jnp.int32, (16, 128), 0)
    lane16 = lax.broadcasted_iota(jnp.int32, (16, 128), 1)
    freq = row16 * 128 + lane16
    phase = ((freq * delay) & (WIDE - 1)).astype(jnp.float32) * (-math.pi / HALF)
    cos_rot, sin_rot = jnp.cos(phase), jnp.sin(phase)
    re, im = strain_ref[0:16, :], strain_ref[16:32, :]
    lane1 = lax.broadcasted_iota(jnp.int32, (1, 128), 1)
    for c, x in enumerate((re * cos_rot - im * sin_rot, re * sin_rot + im * cos_rot)):
        x = to_classes([x[g : g + 1, :] for g in range(16)], lane1)
        for f2 in range(CLASSES):
            at = f2 * 256 + c * 128
            packet_ref[0, :, at : at + 128] = x[f2]
    shifted = packet_ref[0, :, 0:WIDE]
    for m in range(PEERS * ND):
        if m:
            packet_ref[m, :, 0:WIDE] = shifted
        packet_ref[m, :, WIDE:] = table[m // ND : m // ND + 1, :]


def bank_kernel(dur_ref, bank_ref, out_ref):
    row16 = lax.broadcasted_iota(jnp.int32, (16, 128), 0)
    lane16 = lax.broadcasted_iota(jnp.int32, (16, 128), 1)

    def rows(i, _):
        r = pl.ds(pl.multiple_of(i * 16, 16), 16)
        dur = jnp.zeros((16, 128), jnp.int32)
        for j in range(16):
            dur = jnp.where(row16 == j, dur_ref[0, i * 16 + j], dur)
        for c in range(2):
            x = []
            for g in range(16):
                v = bank_ref[r, c * HALF + g * 128 : c * HALF + (g + 1) * 128].astype(jnp.float32)
                x.append(jnp.where(dur <= g, v, 0.0))
            x = to_classes(x, lane16)
            for f2 in range(CLASSES):
                at = f2 * 256 + c * 128
                out_ref[r, at : at + 128] = x[f2].astype(jnp.bfloat16)
        return 0

    lax.fori_loop(0, SLOTS // 16, rows, 0)


def head(delays, strain, owner, slot):
    n = owner.shape[1]
    vmem = pl.BlockSpec(memory_space=pltpu.VMEM)
    smem = pl.BlockSpec(memory_space=pltpu.SMEM)
    return pl.pallas_call(
        head_kernel,
        out_shape=[
            jax.ShapeDtypeStruct((PEERS * ND, 1, WIDE + 128), jnp.float32),
            jax.ShapeDtypeStruct((n, 8), jnp.float32),
        ],
        in_specs=[smem] + [vmem] * 3,
        out_specs=[vmem] * 2,
        compiler_params=pltpu.CompilerParams(vmem_limit_bytes=58 << 20),
        cost_estimate=pl.CostEstimate(flops=4 << 20, bytes_accessed=2 << 20, transcendentals=0),
        name="head",
    )(delays, strain, owner, slot)


def prepare_bank(dur, bank):
    vmem = pl.BlockSpec(memory_space=pltpu.VMEM)
    return pl.pallas_call(
        bank_kernel,
        out_shape=jax.ShapeDtypeStruct((SLOTS, WIDE), jnp.bfloat16),
        in_specs=[pl.BlockSpec(memory_space=pltpu.SMEM), vmem],
        out_specs=vmem,
        compiler_params=pltpu.CompilerParams(vmem_limit_bytes=58 << 20),
        cost_estimate=pl.CostEstimate(flops=4 << 20, bytes_accessed=2 << 20, transcendentals=0),
        name="prepare_bank",
    )(dur, bank)


def combine_kernel(antenna_ref, packet_ref, out_ref):
    det = lax.axis_index("det")
    for s in range(PEERS):
        rows = [packet_ref[s * ND + d, :, 0:WIDE] for d in range(ND)]
        for p in range(2):
            total = antenna_ref[p, 0] * rows[0]
            for d in range(1, ND):
                total = total + antenna_ref[p, d] * rows[d]
            out_ref[s, :, p * WIDE : (p + 1) * WIDE] = total
        out_ref[s, :, 2 * WIDE :] = packet_ref[s * ND + det, :, WIDE:]


def combine(antenna, packet):
    vmem = pl.BlockSpec(memory_space=pltpu.VMEM)
    smem = pl.BlockSpec(memory_space=pltpu.SMEM)
    return pl.pallas_call(
        combine_kernel,
        out_shape=jax.ShapeDtypeStruct((PEERS, 1, 2 * WIDE + 128), jnp.float32),
        in_specs=[smem, vmem],
        out_specs=vmem,
        compiler_params=pltpu.CompilerParams(vmem_limit_bytes=16 << 20),
        cost_estimate=pl.CostEstimate(flops=1 << 20, bytes_accessed=1 << 20, transcendentals=0),
        name="combine",
    )(antenna, packet)


def rotate(re, im, k):
    k %= 16
    if k == 0:
        return re, im
    if k == 4:
        return -im, re
    if k == 8:
        return -re, -im
    if k == 12:
        return im, -re
    c, s = math.cos(math.pi * k / 8), math.sin(math.pi * k / 8)
    return re * c - im * s, re * s + im * c


def cadd(a, b):
    return a[0] + b[0], a[1] + b[1]


def csub(a, b):
    return a[0] - b[0], a[1] - b[1]


def lags_of(load):
    def four(a):
        x0, x1, x2, x3 = load(a), load(a + 4), load(a + 8), load(a + 12)
        e0, e1, o0, o1 = cadd(x0, x2), csub(x0, x2), cadd(x1, x3), csub(x1, x3)
        turned = (-o1[1], o1[0])
        return [cadd(e0, o0), cadd(e1, turned), csub(e0, o0), csub(e1, turned)]

    def pair(a):
        y, z = four(a), four(a + 2)
        return [cadd(y[q], rotate(*z[q], 2 * q)) for q in range(QS)]

    even, odd = pair(0), pair(1)
    return [cadd(even[q], rotate(*odd[q], q)) for q in range(QS)]


def stage_kernel(source, out_ref, sem):
    copy = pltpu.make_async_copy(source, out_ref, sem)
    copy.start()
    copy.wait()


def stage(basis):
    return pl.pallas_call(
        stage_kernel,
        out_shape=jax.ShapeDtypeStruct(basis.shape, basis.dtype),
        in_specs=[pl.BlockSpec(memory_space=pl.ANY)],
        out_specs=pl.BlockSpec(memory_space=pltpu.VMEM),
        scratch_shapes=[pltpu.SemaphoreType.DMA],
        compiler_params=pltpu.CompilerParams(vmem_limit_bytes=16 << 20),
        cost_estimate=pl.CostEstimate(flops=0, bytes_accessed=8 << 20, transcendentals=0),
        name="stage_basis",
    )(basis)


def filter_kernel(count, first, slot, *refs):
    banks = refs[:count]
    packet_ref, basis_ref, _, whole_ref, token_ref, bank, column, coh, spec, xs, norms, out_ref, bank_sems, out_sem = refs[count:]
    half = PEERS * CAP
    loads = [pltpu.make_async_copy(banks[i], bank.at[i], bank_sems.at[i]) for i in range(count)]
    for load in loads:
        load.start()
    table = jnp.concatenate([packet_ref[s, :, 2 * WIDE : 2 * WIDE + 128] for s in range(PEERS)], 0)
    column[...] = jnp.transpose(table)
    for s in range(PEERS):
        for p in range(2):
            coh[2 * s + p : 2 * s + p + 1, :] = packet_ref[s, :, p * WIDE : (p + 1) * WIDE]
    lane = lax.broadcasted_iota(jnp.int32, (CAP, SLOTS), 1).astype(jnp.float32)

    def block(i, _):
        for j in range(count):

            @pl.when(i == j)
            def _(j=j):
                loads[j].wait()

        want = column[pl.ds(pl.multiple_of(first + i * CAP, CAP), CAP), :]
        hot = jnp.concatenate(
            [(want[:, s : s + 1] == lane).astype(jnp.float32) for s in range(PEERS)], 0
        ).astype(jnp.bfloat16)
        for f2 in range(CLASSES):
            at = f2 * 256
            xs[f2, :half, :256] = jnp.dot(
                hot, bank[i, :, at : at + 256], preferred_element_type=jnp.float32
            )
        square = jnp.zeros((half, 128), jnp.float32)
        for f2 in range(CLASSES):
            at = f2 * 256
            tr, ti = xs[f2, :half, :128], xs[f2, :half, 128:256]
            square = square + (tr * tr + ti * ti)
            for s in range(PEERS):
                rs = slice(s * CAP, (s + 1) * CAP)
                trs, tis = tr[rs], ti[rs]
                for p in range(2):
                    nr = coh[2 * s + p : 2 * s + p + 1, at : at + 128]
                    ni = coh[2 * s + p : 2 * s + p + 1, at + 128 : at + 256]
                    to = slice(p * half + s * CAP, p * half + (s + 1) * CAP)
                    spec[f2, to, 0:128] = (nr * trs + ni * tis).astype(jnp.bfloat16)
                    spec[f2, to, 128:256] = (ni * trs - nr * tis).astype(jnp.bfloat16)
        norms[...] = jnp.broadcast_to(jnp.sum(square, axis=1, keepdims=True), (half, 128))

        for f2 in range(CLASSES):
            xs[f2] = jnp.dot(spec[f2], basis_ref[f2], preferred_element_type=jnp.float32)

        def tile(s, _):
            row = pl.multiple_of(s * CAP, CAP)
            norm = norms[pl.ds(row, CAP), :]
            good = norm > 0.0
            scale = jnp.where(good, 1.0 / jnp.where(good, norm, 1.0), 0.0)
            offset = jnp.where(good, 0.0, -1.0)
            for h in range(T1 // 128):
                parts = [[] for _ in range(QS)]
                for u in range(CAP // 8):
                    power = [None] * QS
                    for p in range(2):
                        rows = pl.ds(p * half + row + 8 * u, 8)

                        def load(f2, rows=rows, h=h):
                            return (
                                xs[f2, rows, h * 128 : (h + 1) * 128],
                                xs[f2, rows, T1 + h * 128 : T1 + (h + 1) * 128],
                            )

                        for q, (re, im) in enumerate(lags_of(load)):
                            w = re * re + im * im
                            power[q] = w if p == 0 else power[q] + w
                    for q in range(QS):
                        v = power[q] * scale[8 * u : 8 * u + 8] + offset[8 * u : 8 * u + 8]
                        parts[q].append(jnp.minimum(v, BIG))
                for q in range(QS):
                    v = jnp.concatenate(parts[q], 0).astype(jnp.bfloat16)
                    out_ref[s, i, :, q * T1 + h * 128 : q * T1 + (h + 1) * 128] = v
            return 0

        lax.fori_loop(0, PEERS, tile, 0, unroll=2)
        return 0

    lax.fori_loop(0, count, block, 0)
    put = pltpu.make_async_copy(out_ref, whole_ref.at[:, pl.ds(slot, count)], out_sem)
    put.start()
    token_ref[...] = norms[0:8, :]
    put.wait()


def filter_banks(banks, first, packet, basis, slot, total, before):
    count = len(banks)
    vmem = pl.BlockSpec(memory_space=pltpu.VMEM)
    any_space = pl.BlockSpec(memory_space=pl.ANY)
    half = PEERS * CAP
    return pl.pallas_call(
        functools.partial(filter_kernel, count, first, slot),
        out_shape=[
            jax.ShapeDtypeStruct((PEERS, total, CAP, STEP), jnp.bfloat16),
            jax.ShapeDtypeStruct((8, 128), jnp.float32),
        ],
        in_specs=[any_space] * count + [vmem, vmem, any_space],
        out_specs=[any_space, vmem],
        input_output_aliases={count + 2: 0} if slot else {},
        scratch_shapes=[
            pltpu.VMEM((count, SLOTS, WIDE), jnp.bfloat16),
            pltpu.VMEM((128, PEERS), jnp.float32),
            pltpu.VMEM((2 * PEERS, WIDE), jnp.float32),
            pltpu.VMEM((CLASSES, 2 * half, 256), jnp.bfloat16),
            pltpu.VMEM((CLASSES, 2 * half, 2 * T1), jnp.float32),
            pltpu.VMEM((half, 128), jnp.float32),
            pltpu.VMEM((PEERS, count, CAP, STEP), jnp.bfloat16),
            pltpu.SemaphoreType.DMA((count,)),
            pltpu.SemaphoreType.DMA,
        ],
        compiler_params=pltpu.CompilerParams(vmem_limit_bytes=24 << 20),
        cost_estimate=pl.CostEstimate(
            flops=count * (3 << 30), bytes_accessed=(5 << 20) + count * (1 << 20), transcendentals=0
        ),
        name=f"filter{count}_{first}",
    )(*banks, packet, basis, before)


def order_kernel(sizes, *refs):
    rows = refs[: len(sizes)]
    place_ref, out_ref = refs[len(sizes) :]
    out, first = None, 0
    for n, ref in zip(sizes, rows):
        lane = first + lax.broadcasted_iota(jnp.int32, (place_ref.shape[0], n), 1)
        pick = (place_ref[:, 0:1] == lane.astype(jnp.float32)).astype(jnp.bfloat16)
        part = jnp.dot(pick, ref[...], preferred_element_type=jnp.float32)
        out = part if out is None else out + part
        first += n
    out_ref[...] = jnp.where(out < 0.0, jnp.nan, out)


def order_rows(rows, place):
    n = place.shape[0]
    step = 128
    return pl.pallas_call(
        functools.partial(order_kernel, [r.shape[0] for r in rows]),
        out_shape=jax.ShapeDtypeStruct((n, STEP), jnp.float32),
        grid=(n // step,),
        in_specs=[pl.BlockSpec(r.shape, lambda i: (0, 0)) for r in rows]
        + [pl.BlockSpec((step, 8), lambda i: (i, 0))],
        out_specs=pl.BlockSpec((step, STEP), lambda i: (i, 0)),
        compiler_params=pltpu.CompilerParams(vmem_limit_bytes=24 << 20),
        cost_estimate=pl.CostEstimate(flops=1 << 30, bytes_accessed=4 << 20, transcendentals=0),
        name="order_rows",
    )(*rows, place)


def per_device(basis, strain, antenna, delays, template_bank, duration_bin, owner_seg, slot_index):
    def at(x, z, c):
        return (x * NZ + z) * NC + c

    places = [(x, z, c) for x in range(NX) for z in range(NZ) for c in range(NC)]
    groups = [[at(x, z, c) for x in range(NX) for c in range(NC)] for z in range(NZ)]
    up = [(at(x, z, c), at(x, (z + 1) % NZ, c)) for x, z, c in places]
    down = [(at(x, z, c), at(x, (z - 1) % NZ, c)) for x, z, c in places]
    groups = [[i * ND + d for i in group for d in range(ND)] for group in groups]
    back_groups = [[at(x, z, c) for x in range(NX) for c in range(NC)] for z in range(NZ)]
    half = SLOTS // 2

    with jax.named_scope("head"):
        own = prepare_bank(duration_bin, template_bank[0])
        own, strain = lax.optimization_barrier((own, strain))
        packet, place = head(
            delays, strain.reshape(WIDE // 128, 128), owner_seg.reshape(1, -1), slot_index
        )

    held = {0: own}

    def ring(k):
        with jax.named_scope("ring"):
            if k < 4:
                held[-k] = lax.ppermute(held[1 - k], "seg", up)
                held[k] = lax.ppermute(held[k - 1], "seg", down)
            else:
                held[4] = jnp.concatenate(
                    [lax.ppermute(held[-3][:half], "seg", up), lax.ppermute(held[3][half:], "seg", down)], 0
                )

    ring(1)
    with jax.named_scope("exchange"):
        packet = lax.all_to_all(
            packet, ("seg", "det"), split_axis=0, concat_axis=0, tiled=True, axis_index_groups=groups
        )
        packet, held[1], held[-1] = lax.optimization_barrier((packet, held[1], held[-1]))
        packet = combine(antenna, packet)
        basis = stage(basis)
    ring(2)

    back, first, token = [], 0, place
    for part in PARTS:
        m = len(part)
        rows, slot = token, 0
        for step in CALLS[part]:
            with jax.named_scope("filter"):
                rows, token = filter_banks(
                    [held[d] for d in step], first + slot * CAP, packet, basis, slot, m, rows
                )
            slot += len(step)
            k = max(held)
            if k < 4:
                token, held[k], held[-k] = lax.optimization_barrier((token, held[k], held[-k]))
                ring(k + 1)
        first += m * CAP
        with jax.named_scope("back"):
            rows = lax.all_to_all(
                rows.reshape(PEERS, m * CAP, STEP),
                "seg",
                split_axis=0,
                concat_axis=0,
                tiled=True,
                axis_index_groups=back_groups,
            )
        back.append(rows.reshape(PEERS * m * CAP, STEP))
    with jax.named_scope("order"):
        return order_rows(back, place)[None]


def solution(mesh):
    basis = class_basis()
    in_specs = (
        P("det", "seg", None),
        P(),
        P(),
        P("seg", "det", None),
        P("seg", "det"),
        P("seg", "det", None),
        P("seg", "det"),
    )

    def run(*args):
        return jax.shard_map(
            lambda *a: per_device(jnp.asarray(basis), *a),
            mesh=mesh,
            in_specs=in_specs,
            out_specs=P("seg", "det", None),
            check_vma=False,
        )(*args)

    return run
```

```python
import functools
import math

import jax
import jax.numpy as jnp
import numpy as np
from jax import lax
from jax.experimental import pallas as pl
from jax.experimental.pallas import tpu as pltpu
from jax.sharding import PartitionSpec as P

HALF = 2048
WIDE = 2 * HALF
STEP = 1024
NX, NZ, NC = 4, 8, 2
PEERS = NX * NC
ND = 4
CAP = 16
SLOTS = 64
CLASSES = 16
T1 = 256
QS = 4
BIG = 3.0e38
CALLS = {(0, -1, 1, -2, 2): ((0, -1, 1), (-2, 2)), (-3, 3, 4): ((-3, 3, 4),)}
PARTS = tuple(CALLS)

LANE = np.arange(128)
FREQ = 128 * (LANE % 16)[None, :] + 16 * (LANE // 16)[None, :] + np.arange(CLASSES)[:, None]


def class_basis():
    t = np.arange(T1)
    ang = ((FREQ[:, :, None] * t[None, None, :]) % WIDE) * (math.pi / HALF)
    c, s = np.cos(ang), np.sin(ang)
    upper = np.concatenate([c, s], 2)
    lower = np.concatenate([-s, c], 2)
    return np.concatenate([upper, lower], 1).astype(np.float32).astype(jnp.bfloat16)


def to_classes(x, lane):
    for k in range(4):
        b = 1 << k
        up = (lane & b) != 0
        for g in range(16):
            if g & b:
                continue
            lo, hi = x[g], x[g | b]
            x[g] = jnp.where(up, pltpu.roll(hi, b, 1), lo)
            x[g | b] = jnp.where(up, hi, pltpu.roll(lo, 128 - b, 1))
    return x


def lookup(dz, values):
    out = jnp.zeros_like(dz)
    for d, v in enumerate(values):
        if v:
            out = jnp.where(dz == d, v, out)
    return out


def head_kernel(delays_ref, strain_ref, owner_ref, slot_ref, packet_ref, place_ref):
    det, my_z = lax.axis_index("det"), (lax.axis_index("seg") // NC) % NZ
    owner = owner_ref[...]
    n = owner.shape[1]
    peer = (owner // (NZ * NC)) * NC + (owner & 1)
    dz = ((owner >> 1) - my_z) & (NZ - 1)
    part_of, order_of, first_of = [0] * NZ, [0] * NZ, [0] * NZ
    first = 0
    for g, part in enumerate(PARTS):
        for j, d in enumerate(part):
            part_of[d % NZ], order_of[d % NZ], first_of[d % NZ] = g, j, first
        first += len(part) * CAP
    hot = owner == lax.broadcasted_iota(jnp.int32, (PEERS * NZ, n), 0)
    earlier = lax.broadcasted_iota(jnp.int32, (n, n), 0) < lax.broadcasted_iota(jnp.int32, (n, n), 1)
    before = jnp.dot(
        hot.astype(jnp.float32).astype(jnp.bfloat16),
        earlier.astype(jnp.float32).astype(jnp.bfloat16),
        preferred_element_type=jnp.float32,
    )
    rank = jnp.sum(jnp.where(hot, before, 0.0), axis=0, keepdims=True).astype(jnp.int32)
    start = lookup(dz, first_of)
    rank = rank + CAP * lookup(dz, order_of)
    want = (slot_ref[...] + 1).astype(jnp.float32)
    size = lookup(dz, [len(PARTS[g]) * CAP for g in part_of])
    place = (start * PEERS + peer * size + rank).astype(jnp.float32)
    place_ref[...] = jnp.broadcast_to(place, (8, n))
    wanted = jnp.where(peer == lax.broadcasted_iota(jnp.int32, (PEERS, n), 0), want, 0.0)
    spot = (start + rank) == lax.broadcasted_iota(jnp.int32, (NZ * CAP, n), 0)
    table = (
        lax.dot_general(
            wanted.astype(jnp.bfloat16),
            spot.astype(jnp.float32).astype(jnp.bfloat16),
            (((1,), (1,)), ((), ())),
            preferred_element_type=jnp.float32,
        )
        - 1.0
    )

    delay = delays_ref[det]
    row16 = lax.broadcasted_iota(jnp.int32, (16, 128), 0)
    lane16 = lax.broadcasted_iota(jnp.int32, (16, 128), 1)
    freq = row16 * 128 + lane16
    phase = ((freq * delay) & (WIDE - 1)).astype(jnp.float32) * (-math.pi / HALF)
    cos_rot, sin_rot = jnp.cos(phase), jnp.sin(phase)
    re, im = strain_ref[0:16, :], strain_ref[16:32, :]
    lane1 = lax.broadcasted_iota(jnp.int32, (1, 128), 1)
    for c, x in enumerate((re * cos_rot - im * sin_rot, re * sin_rot + im * cos_rot)):
        x = to_classes([x[g : g + 1, :] for g in range(16)], lane1)
        for f2 in range(CLASSES):
            at = f2 * 256 + c * 128
            packet_ref[0, :, at : at + 128] = x[f2]
    shifted = packet_ref[0, :, 0:WIDE]
    for m in range(PEERS * ND):
        if m:
            packet_ref[m, :, 0:WIDE] = shifted
        packet_ref[m, :, WIDE:] = table[m // ND : m // ND + 1, :]


def bank_kernel(dur_ref, bank_ref, out_ref):
    row16 = lax.broadcasted_iota(jnp.int32, (16, 128), 0)
    lane16 = lax.broadcasted_iota(jnp.int32, (16, 128), 1)

    def rows(i, _):
        r = pl.ds(pl.multiple_of(i * 16, 16), 16)
        dur = jnp.zeros((16, 128), jnp.int32)
        for j in range(16):
            dur = jnp.where(row16 == j, dur_ref[0, i * 16 + j], dur)
        for c in range(2):
            x = []
            for g in range(16):
                v = bank_ref[r, c * HALF + g * 128 : c * HALF + (g + 1) * 128].astype(jnp.float32)
                x.append(jnp.where(dur <= g, v, 0.0))
            x = to_classes(x, lane16)
            for f2 in range(CLASSES):
                at = f2 * 256 + c * 128
                out_ref[r, at : at + 128] = x[f2].astype(jnp.bfloat16)
        return 0

    lax.fori_loop(0, SLOTS // 16, rows, 0)


def head(delays, strain, owner, slot):
    n = owner.shape[1]
    vmem = pl.BlockSpec(memory_space=pltpu.VMEM)
    smem = pl.BlockSpec(memory_space=pltpu.SMEM)
    return pl.pallas_call(
        head_kernel,
        out_shape=[
            jax.ShapeDtypeStruct((PEERS * ND, 1, WIDE + 128), jnp.float32),
            jax.ShapeDtypeStruct((8, n), jnp.float32),
        ],
        in_specs=[smem] + [vmem] * 3,
        out_specs=[vmem] * 2,
        compiler_params=pltpu.CompilerParams(vmem_limit_bytes=58 << 20),
        cost_estimate=pl.CostEstimate(flops=4 << 20, bytes_accessed=2 << 20, transcendentals=0),
        name="head",
    )(delays, strain, owner, slot)


def prepare_bank(dur, bank):
    vmem = pl.BlockSpec(memory_space=pltpu.VMEM)
    return pl.pallas_call(
        bank_kernel,
        out_shape=jax.ShapeDtypeStruct((SLOTS, WIDE), jnp.bfloat16),
        in_specs=[pl.BlockSpec(memory_space=pltpu.SMEM), vmem],
        out_specs=vmem,
        compiler_params=pltpu.CompilerParams(vmem_limit_bytes=58 << 20),
        cost_estimate=pl.CostEstimate(flops=8 << 30, bytes_accessed=2 << 20, transcendentals=0),
        name="prepare_bank",
    )(dur, bank)


def combine_kernel(antenna_ref, packet_ref, out_ref):
    det = lax.axis_index("det")
    for s in range(PEERS):
        rows = [packet_ref[s * ND + d, :, 0:WIDE] for d in range(ND)]
        for p in range(2):
            total = antenna_ref[p, 0] * rows[0]
            for d in range(1, ND):
                total = total + antenna_ref[p, d] * rows[d]
            out_ref[s, :, p * WIDE : (p + 1) * WIDE] = total
        out_ref[s, :, 2 * WIDE :] = packet_ref[s * ND + det, :, WIDE:]


def combine(antenna, packet):
    vmem = pl.BlockSpec(memory_space=pltpu.VMEM)
    smem = pl.BlockSpec(memory_space=pltpu.SMEM)
    return pl.pallas_call(
        combine_kernel,
        out_shape=jax.ShapeDtypeStruct((PEERS, 1, 2 * WIDE + 128), jnp.float32),
        in_specs=[smem, vmem],
        out_specs=vmem,
        compiler_params=pltpu.CompilerParams(vmem_limit_bytes=16 << 20),
        cost_estimate=pl.CostEstimate(flops=1 << 20, bytes_accessed=1 << 20, transcendentals=0),
        name="combine",
    )(antenna, packet)


def rotate(re, im, k):
    k %= 16
    if k == 0:
        return re, im
    if k == 4:
        return -im, re
    if k == 8:
        return -re, -im
    if k == 12:
        return im, -re
    r = math.sqrt(0.5)
    if k == 2:
        return (re - im) * r, (re + im) * r
    if k == 6:
        return (re + im) * -r, (re - im) * r
    c, s = math.cos(math.pi * k / 8), math.sin(math.pi * k / 8)
    return re * c - im * s, re * s + im * c


def cadd(a, b):
    return a[0] + b[0], a[1] + b[1]


def csub(a, b):
    return a[0] - b[0], a[1] - b[1]


def lags_of(load):
    def four(a):
        x0, x1, x2, x3 = load(a), load(a + 4), load(a + 8), load(a + 12)
        e0, e1, o0, o1 = cadd(x0, x2), csub(x0, x2), cadd(x1, x3), csub(x1, x3)
        turned = (-o1[1], o1[0])
        return [cadd(e0, o0), cadd(e1, turned), csub(e0, o0), csub(e1, turned)]

    def pair(a):
        y, z = four(a), four(a + 2)
        return [cadd(y[q], rotate(*z[q], 2 * q)) for q in range(QS)]

    even, odd = pair(0), pair(1)
    return [cadd(even[q], rotate(*odd[q], q)) for q in range(QS)]


def stage_kernel(source, out_ref, sem):
    copy = pltpu.make_async_copy(source, out_ref, sem)
    copy.start()
    copy.wait()


def stage(basis):
    return pl.pallas_call(
        stage_kernel,
        out_shape=jax.ShapeDtypeStruct(basis.shape, basis.dtype),
        in_specs=[pl.BlockSpec(memory_space=pl.ANY)],
        out_specs=pl.BlockSpec(memory_space=pltpu.VMEM),
        scratch_shapes=[pltpu.SemaphoreType.DMA],
        compiler_params=pltpu.CompilerParams(vmem_limit_bytes=16 << 20),
        cost_estimate=pl.CostEstimate(flops=0, bytes_accessed=8 << 20, transcendentals=0),
        name="stage_basis",
    )(basis)


def filter_kernel(count, first, slot, spread, *refs):
    banks = refs[:count]
    packet_ref, basis_ref, _, *outs, token_ref, bank, column, coh, spec, xs, norms, out_ref, bank_sems, out_sem = refs[count:]
    half = PEERS * CAP
    loads = [pltpu.make_async_copy(banks[i], bank.at[i], bank_sems.at[i]) for i in range(count)]
    for load in loads:
        load.start()
    table = jnp.concatenate([packet_ref[s, :, 2 * WIDE : 2 * WIDE + 128] for s in range(PEERS)], 0)
    column[...] = jnp.transpose(table)
    for s in range(PEERS):
        for p in range(2):
            coh[2 * s + p : 2 * s + p + 1, :] = packet_ref[s, :, p * WIDE : (p + 1) * WIDE]
    lane = lax.broadcasted_iota(jnp.int32, (CAP, SLOTS), 1).astype(jnp.float32)

    def block(i, _):
        for j in range(count):

            @pl.when(i == j)
            def _(j=j):
                loads[j].wait()

        want = column[pl.ds(pl.multiple_of(first + i * CAP, CAP), CAP), :]
        hot = jnp.concatenate(
            [(want[:, s : s + 1] == lane).astype(jnp.float32) for s in range(PEERS)], 0
        ).astype(jnp.bfloat16)
        for f2 in range(CLASSES):
            at = f2 * 256
            xs[f2, :half, :256] = jnp.dot(
                hot, bank[i, :, at : at + 256], preferred_element_type=jnp.float32
            )
        square = jnp.zeros((half, 128), jnp.float32)
        for f2 in range(CLASSES):
            at = f2 * 256
            tr, ti = xs[f2, :half, :128], xs[f2, :half, 128:256]
            square = square + (tr * tr + ti * ti)
            for s in range(PEERS):
                rs = slice(s * CAP, (s + 1) * CAP)
                trs, tis = tr[rs], ti[rs]
                for p in range(2):
                    nr = coh[2 * s + p : 2 * s + p + 1, at : at + 128]
                    ni = coh[2 * s + p : 2 * s + p + 1, at + 128 : at + 256]
                    to = slice(p * half + s * CAP, p * half + (s + 1) * CAP)
                    spec[f2, to, 0:128] = (nr * trs + ni * tis).astype(jnp.bfloat16)
                    spec[f2, to, 128:256] = (ni * trs - nr * tis).astype(jnp.bfloat16)
        norms[...] = jnp.broadcast_to(jnp.sum(square, axis=1, keepdims=True), (half, 128))

        for f2 in range(CLASSES):
            xs[f2] = jnp.dot(spec[f2], basis_ref[f2], preferred_element_type=jnp.float32)

        def tile(s, _):
            row = pl.multiple_of(s * CAP, CAP)
            norm = norms[pl.ds(row, CAP), :]
            good = norm > 0.0
            scale = jnp.where(good, 1.0 / jnp.where(good, norm, 1.0), 0.0)
            offset = jnp.where(good, 0.0, -1.0)
            for h in range(T1 // 128):
                parts = [[] for _ in range(QS)]
                for u in range(CAP // 8):
                    power = [None] * QS
                    for p in range(2):
                        rows = pl.ds(p * half + row + 8 * u, 8)

                        def load(f2, rows=rows, h=h):
                            return (
                                xs[f2, rows, h * 128 : (h + 1) * 128],
                                xs[f2, rows, T1 + h * 128 : T1 + (h + 1) * 128],
                            )

                        for q, (re, im) in enumerate(lags_of(load)):
                            w = re * re + im * im
                            power[q] = w if p == 0 else power[q] + w
                    for q in range(QS):
                        v = power[q] * scale[8 * u : 8 * u + 8] + offset[8 * u : 8 * u + 8]
                        parts[q].append(jnp.minimum(v, BIG))
                for q in range(QS):
                    v = jnp.concatenate(parts[q], 0).astype(jnp.bfloat16)
                    out_ref[s, i, :, q * T1 + h * 128 : q * T1 + (h + 1) * 128] = v
            return 0

        lax.fori_loop(0, PEERS, tile, 0, unroll=2)
        return 0

    lax.fori_loop(0, count, block, 0)
    if spread:
        x, c = lax.axis_index("seg") // (NZ * NC), lax.axis_index("seg") % NC
        puts = [
            pltpu.make_async_copy(
                out_ref.at[((x + dx) % NX) * NC + (c + dc) % NC], outs[dx * NC + dc], out_sem.at[dx * NC + dc]
            )
            for dx in range(NX)
            for dc in range(NC)
        ]
    else:
        puts = [pltpu.make_async_copy(out_ref, outs[0].at[:, pl.ds(slot, count)], out_sem.at[0])]
    for put in puts:
        put.start()
    token_ref[...] = norms[0:8, :]
    for put in puts:
        put.wait()


def filter_banks(banks, first, packet, basis, slot, total, before, spread=False):
    count = len(banks)
    vmem = pl.BlockSpec(memory_space=pltpu.VMEM)
    any_space = pl.BlockSpec(memory_space=pl.ANY)
    half = PEERS * CAP
    return pl.pallas_call(
        functools.partial(filter_kernel, count, first, slot, spread),
        out_shape=[
            jax.ShapeDtypeStruct(shape, jnp.bfloat16)
            for shape in ([(count, CAP, STEP)] * PEERS if spread else [(PEERS, total, CAP, STEP)])
        ]
        + [jax.ShapeDtypeStruct((8, 128), jnp.float32)],
        in_specs=[any_space] * count + [vmem, vmem, any_space],
        out_specs=[any_space] * (PEERS if spread else 1) + [vmem],
        input_output_aliases={count + 2: 0} if slot else {},
        scratch_shapes=[
            pltpu.VMEM((count, SLOTS, WIDE), jnp.bfloat16),
            pltpu.VMEM((128, PEERS), jnp.float32),
            pltpu.VMEM((2 * PEERS, WIDE), jnp.float32),
            pltpu.VMEM((CLASSES, 2 * half, 256), jnp.bfloat16),
            pltpu.VMEM((CLASSES, 2 * half, 2 * T1), jnp.float32),
            pltpu.VMEM((half, 128), jnp.float32),
            pltpu.VMEM((PEERS, count, CAP, STEP), jnp.bfloat16),
            pltpu.SemaphoreType.DMA((count,)),
            pltpu.SemaphoreType.DMA((PEERS,)),
        ],
        compiler_params=pltpu.CompilerParams(vmem_limit_bytes=24 << 20),
        cost_estimate=pl.CostEstimate(
            flops=0 if spread else count * (3 << 30), bytes_accessed=1 << 20, transcendentals=0
        ),
        name=f"filter{count}_{first}",
    )(*banks, packet, basis, before)


def order_kernel(near_ref, *refs):
    *pieces, place_ref, out_ref, far = refs
    count = pieces[0].shape[0]
    x, c = lax.axis_index("seg") // (NZ * NC), lax.axis_index("seg") % NC

    @pl.when(pl.program_id(0) == 0)
    def _():
        for dx in range(NX):
            for dc in range(NC):
                peer = ((x + NX - dx) % NX) * NC + (c + dc) % NC
                rows = pl.ds(pl.multiple_of(peer * count, CAP), count)
                far[rows, :] = pieces[dx * NC + dc][...]

    column = jnp.transpose(place_ref[...])[:, 0:1]
    out, first = None, 0
    for ref in (near_ref, far):
        n = ref.shape[0]
        lane = (first + lax.broadcasted_iota(jnp.int32, (column.shape[0], n), 1)).astype(jnp.float32)
        pick = (column == lane).astype(jnp.bfloat16)
        part = jnp.dot(pick, ref[...], preferred_element_type=jnp.float32)
        out = part if out is None else out + part
        first += n
    out_ref[...] = jnp.where(out < 0.0, jnp.nan, out)


def order_rows(near, pieces, place):
    n = place.shape[1]
    step = 128
    whole = [pl.BlockSpec(r.shape, lambda i: (0, 0)) for r in [near, *pieces]]
    return pl.pallas_call(
        order_kernel,
        out_shape=jax.ShapeDtypeStruct((n, STEP), jnp.float32),
        grid=(n // step,),
        in_specs=whole + [pl.BlockSpec((8, step), lambda i: (0, i))],
        out_specs=pl.BlockSpec((step, STEP), lambda i: (i, 0)),
        scratch_shapes=[pltpu.VMEM((PEERS * pieces[0].shape[0], STEP), jnp.bfloat16)],
        compiler_params=pltpu.CompilerParams(vmem_limit_bytes=24 << 20),
        cost_estimate=pl.CostEstimate(flops=1 << 30, bytes_accessed=4 << 20, transcendentals=0),
        name="order_rows",
    )(near, *pieces, place)


def per_device(basis, strain, antenna, delays, template_bank, duration_bin, owner_seg, slot_index):
    def at(x, z, c):
        return (x * NZ + z) * NC + c

    places = [(x, z, c) for x in range(NX) for z in range(NZ) for c in range(NC)]
    groups = [[at(x, z, c) for x in range(NX) for c in range(NC)] for z in range(NZ)]
    up = [(at(x, z, c), at(x, (z + 1) % NZ, c)) for x, z, c in places]
    down = [(at(x, z, c), at(x, (z - 1) % NZ, c)) for x, z, c in places]
    groups = [[i * ND + d for i in group for d in range(ND)] for group in groups]
    back_groups = [[at(x, z, c) for x in range(NX) for c in range(NC)] for z in range(NZ)]
    half = SLOTS // 2

    with jax.named_scope("head"):
        packet, place = head(
            delays, strain.reshape(WIDE // 128, 128), owner_seg.reshape(1, -1), slot_index
        )

    packet, template_bank = lax.optimization_barrier((packet, template_bank))
    with jax.named_scope("bank"):
        own = prepare_bank(duration_bin, template_bank[0])

    held = {0: own}

    def ring(k):
        with jax.named_scope("ring"):
            if k < 4:
                held[-k] = lax.ppermute(held[1 - k], "seg", up)
                held[k] = lax.ppermute(held[k - 1], "seg", down)
            else:
                held[4] = jnp.concatenate(
                    [lax.ppermute(held[-3][:half], "seg", up), lax.ppermute(held[3][half:], "seg", down)], 0
                )

    ring(1)
    with jax.named_scope("exchange"):
        packet = lax.all_to_all(
            packet, ("seg", "det"), split_axis=0, concat_axis=0, tiled=True, axis_index_groups=groups
        )
        packet, held[1], held[-1] = lax.optimization_barrier((packet, held[1], held[-1]))
        packet = combine(antenna, packet)
    ring(2)

    near_part, far_part = PARTS
    rows, slot, token = place, 0, place
    for step in CALLS[near_part]:
        with jax.named_scope("filter"):
            rows, token = filter_banks(
                [held[d] for d in step], slot * CAP, packet, basis, slot, len(near_part), rows
            )
        slot += len(step)
        k = max(held)
        token, held[k], held[-k] = lax.optimization_barrier((token, held[k], held[-k]))
        ring(k + 1)
    with jax.named_scope("back"):
        near = lax.all_to_all(
            rows.reshape(PEERS, slot * CAP, STEP),
            "seg",
            split_axis=0,
            concat_axis=0,
            tiled=True,
            axis_index_groups=back_groups,
        )
    m = len(far_part)
    token, late_basis = lax.optimization_barrier((token, basis))
    late_basis = stage(late_basis)
    with jax.named_scope("filter"):
        *pieces, token = filter_banks(
            [held[d] for d in far_part], slot * CAP, packet, late_basis, 0, m, token, spread=True
        )
    with jax.named_scope("back"):
        for k in range(1, PEERS):
            dx, dc = divmod(k, NC)
            to = [(at(x, z, c), at((x + dx) % NX, z, (c + dc) % NC)) for x, z, c in places]
            pieces[k] = lax.ppermute(pieces[k], "seg", to)
    with jax.named_scope("order"):
        near = near.reshape(PEERS * slot * CAP, STEP)
        return order_rows(near, [p.reshape(m * CAP, STEP) for p in pieces], place)[None]


def solution(mesh):
    basis = class_basis()
    in_specs = (
        P("det", "seg", None),
        P(),
        P(),
        P("seg", "det", None),
        P("seg", "det"),
        P("seg", "det", None),
        P("seg", "det"),
    )

    def run(*args):
        return jax.shard_map(
            lambda *a: per_device(jnp.asarray(basis), *a),
            mesh=mesh,
            in_specs=in_specs,
            out_specs=P("seg", "det", None),
            check_vma=False,
        )(*args)

    return run
```

```python
import functools
import math

import jax
import jax.numpy as jnp
import numpy as np
from jax import lax
from jax.experimental import pallas as pl
from jax.experimental.pallas import tpu as pltpu
from jax.sharding import PartitionSpec as P

HALF = 2048
WIDE = 2 * HALF
STEP = 1024
NX, NZ, NC = 4, 8, 2
PEERS = NX * NC
ND = 4
CAP = 16
SLOTS = 64
CLASSES = 16
T1 = 256
QS = 4
BIG = 3.0e38
CALLS = {(0, -1, 1, -2, 2): ((0, -1, 1), (-2, 2)), (-3, 3, 4): ((-3, 3, 4),)}
PARTS = tuple(CALLS)

LANE = np.arange(128)
FREQ = 128 * (LANE % 16)[None, :] + 16 * (LANE // 16)[None, :] + np.arange(CLASSES)[:, None]


def class_basis():
    t = np.arange(T1)
    ang = ((FREQ[:, :, None] * t[None, None, :]) % WIDE) * (math.pi / HALF)
    c, s = np.cos(ang), np.sin(ang)
    upper = np.concatenate([c, s], 2)
    lower = np.concatenate([-s, c], 2)
    return np.concatenate([upper, lower], 1).astype(np.float32).astype(jnp.bfloat16)


def to_classes(x, lane):
    for k in range(4):
        b = 1 << k
        up = (lane & b) != 0
        for g in range(16):
            if g & b:
                continue
            lo, hi = x[g], x[g | b]
            x[g] = jnp.where(up, pltpu.roll(hi, b, 1), lo)
            x[g | b] = jnp.where(up, hi, pltpu.roll(lo, 128 - b, 1))
    return x


def lookup(dz, values):
    out = jnp.zeros_like(dz)
    for d, v in enumerate(values):
        if v:
            out = jnp.where(dz == d, v, out)
    return out


def head_kernel(
    dur_ref, delays_ref, bank_ref, strain_ref, owner_ref, slot_ref, own_ref, packet_ref, place_ref
):
    det, my_z = lax.axis_index("det"), (lax.axis_index("seg") // NC) % NZ
    owner = owner_ref[...]
    n = owner.shape[1]
    peer = (owner // (NZ * NC)) * NC + (owner & 1)
    dz = ((owner >> 1) - my_z) & (NZ - 1)
    part_of, order_of, first_of = [0] * NZ, [0] * NZ, [0] * NZ
    first = 0
    for g, part in enumerate(PARTS):
        for j, d in enumerate(part):
            part_of[d % NZ], order_of[d % NZ], first_of[d % NZ] = g, j, first
        first += len(part) * CAP
    hot = owner == lax.broadcasted_iota(jnp.int32, (PEERS * NZ, n), 0)
    earlier = lax.broadcasted_iota(jnp.int32, (n, n), 0) < lax.broadcasted_iota(jnp.int32, (n, n), 1)
    before = jnp.dot(
        hot.astype(jnp.float32).astype(jnp.bfloat16),
        earlier.astype(jnp.float32).astype(jnp.bfloat16),
        preferred_element_type=jnp.float32,
    )
    rank = jnp.sum(jnp.where(hot, before, 0.0), axis=0, keepdims=True).astype(jnp.int32)
    start = lookup(dz, first_of)
    rank = rank + CAP * lookup(dz, order_of)
    want = (slot_ref[...] + 1).astype(jnp.float32)
    size = lookup(dz, [len(PARTS[g]) * CAP for g in part_of])
    place = (start * PEERS + peer * size + rank).astype(jnp.float32)
    place_ref[...] = jnp.broadcast_to(place, (8, n))
    wanted = jnp.where(peer == lax.broadcasted_iota(jnp.int32, (PEERS, n), 0), want, 0.0)
    spot = (start + rank) == lax.broadcasted_iota(jnp.int32, (NZ * CAP, n), 0)
    table = (
        lax.dot_general(
            wanted.astype(jnp.bfloat16),
            spot.astype(jnp.float32).astype(jnp.bfloat16),
            (((1,), (1,)), ((), ())),
            preferred_element_type=jnp.float32,
        )
        - 1.0
    )

    delay = delays_ref[det]
    row16 = lax.broadcasted_iota(jnp.int32, (16, 128), 0)
    lane16 = lax.broadcasted_iota(jnp.int32, (16, 128), 1)
    freq = row16 * 128 + lane16
    phase = ((freq * delay) & (WIDE - 1)).astype(jnp.float32) * (-math.pi / HALF)
    cos_rot, sin_rot = jnp.cos(phase), jnp.sin(phase)
    re, im = strain_ref[0:16, :], strain_ref[16:32, :]
    lane1 = lax.broadcasted_iota(jnp.int32, (1, 128), 1)
    for c, x in enumerate((re * cos_rot - im * sin_rot, re * sin_rot + im * cos_rot)):
        x = to_classes([x[g : g + 1, :] for g in range(16)], lane1)
        for f2 in range(CLASSES):
            at = f2 * 256 + c * 128
            packet_ref[0, :, at : at + 128] = x[f2]
    shifted = packet_ref[0, :, 0:WIDE]
    for m in range(PEERS * ND):
        if m:
            packet_ref[m, :, 0:WIDE] = shifted
        packet_ref[m, :, WIDE:] = table[m // ND : m // ND + 1, :]

    def rows(i, _):
        r = pl.ds(pl.multiple_of(i * 16, 16), 16)
        dur = jnp.zeros((16, 128), jnp.int32)
        for j in range(16):
            dur = jnp.where(row16 == j, dur_ref[0, i * 16 + j], dur)
        for c in range(2):
            x = []
            for g in range(16):
                v = bank_ref[r, c * HALF + g * 128 : c * HALF + (g + 1) * 128].astype(jnp.float32)
                x.append(jnp.where(dur <= g, v, 0.0))
            x = to_classes(x, lane16)
            for f2 in range(CLASSES):
                at = f2 * 256 + c * 128
                own_ref[r, at : at + 128] = x[f2].astype(jnp.bfloat16)
        return 0

    lax.fori_loop(0, SLOTS // 16, rows, 0)


def head(dur, delays, bank, strain, owner, slot):
    n = owner.shape[1]
    vmem = pl.BlockSpec(memory_space=pltpu.VMEM)
    smem = pl.BlockSpec(memory_space=pltpu.SMEM)
    return pl.pallas_call(
        head_kernel,
        out_shape=[
            jax.ShapeDtypeStruct((SLOTS, WIDE), jnp.bfloat16),
            jax.ShapeDtypeStruct((PEERS * ND, 1, WIDE + 128), jnp.float32),
            jax.ShapeDtypeStruct((8, n), jnp.float32),
        ],
        in_specs=[smem] * 2 + [vmem] * 4,
        out_specs=[vmem] * 3,
        compiler_params=pltpu.CompilerParams(vmem_limit_bytes=58 << 20),
        cost_estimate=pl.CostEstimate(flops=8 << 30, bytes_accessed=2 << 20, transcendentals=0),
        name="head",
    )(dur, delays, bank, strain, owner, slot)


def combine_kernel(antenna_ref, packet_ref, out_ref):
    det = lax.axis_index("det")
    for s in range(PEERS):
        rows = [packet_ref[s * ND + d, :, 0:WIDE] for d in range(ND)]
        for p in range(2):
            total = antenna_ref[p, 0] * rows[0]
            for d in range(1, ND):
                total = total + antenna_ref[p, d] * rows[d]
            out_ref[s, :, p * WIDE : (p + 1) * WIDE] = total
        out_ref[s, :, 2 * WIDE :] = packet_ref[s * ND + det, :, WIDE:]


def combine(antenna, packet):
    vmem = pl.BlockSpec(memory_space=pltpu.VMEM)
    smem = pl.BlockSpec(memory_space=pltpu.SMEM)
    return pl.pallas_call(
        combine_kernel,
        out_shape=jax.ShapeDtypeStruct((PEERS, 1, 2 * WIDE + 128), jnp.float32),
        in_specs=[smem, vmem],
        out_specs=vmem,
        compiler_params=pltpu.CompilerParams(vmem_limit_bytes=16 << 20),
        cost_estimate=pl.CostEstimate(flops=4 << 30, bytes_accessed=1 << 20, transcendentals=0),
        name="combine",
    )(antenna, packet)


def rotate(re, im, k):
    k %= 16
    if k == 0:
        return re, im
    if k == 4:
        return -im, re
    if k == 8:
        return -re, -im
    if k == 12:
        return im, -re
    r = math.sqrt(0.5)
    if k == 2:
        return (re - im) * r, (re + im) * r
    if k == 6:
        return (re + im) * -r, (re - im) * r
    c, s = math.cos(math.pi * k / 8), math.sin(math.pi * k / 8)
    return re * c - im * s, re * s + im * c


def cadd(a, b):
    return a[0] + b[0], a[1] + b[1]


def csub(a, b):
    return a[0] - b[0], a[1] - b[1]


def lags_of(load):
    def four(a):
        x0, x1, x2, x3 = load(a), load(a + 4), load(a + 8), load(a + 12)
        e0, e1, o0, o1 = cadd(x0, x2), csub(x0, x2), cadd(x1, x3), csub(x1, x3)
        turned = (-o1[1], o1[0])
        return [cadd(e0, o0), cadd(e1, turned), csub(e0, o0), csub(e1, turned)]

    def pair(a):
        y, z = four(a), four(a + 2)
        return [cadd(y[q], rotate(*z[q], 2 * q)) for q in range(QS)]

    even, odd = pair(0), pair(1)
    return [cadd(even[q], rotate(*odd[q], q)) for q in range(QS)]


def stage_kernel(source, out_ref, sem):
    copy = pltpu.make_async_copy(source, out_ref, sem)
    copy.start()
    copy.wait()


def stage(basis):
    return pl.pallas_call(
        stage_kernel,
        out_shape=jax.ShapeDtypeStruct(basis.shape, basis.dtype),
        in_specs=[pl.BlockSpec(memory_space=pl.ANY)],
        out_specs=pl.BlockSpec(memory_space=pltpu.VMEM),
        scratch_shapes=[pltpu.SemaphoreType.DMA],
        compiler_params=pltpu.CompilerParams(vmem_limit_bytes=16 << 20),
        cost_estimate=pl.CostEstimate(flops=0, bytes_accessed=8 << 20, transcendentals=0),
        name="stage_basis",
    )(basis)


def filter_kernel(count, first, slot, spread, *refs):
    banks = refs[:count]
    packet_ref, basis_ref, _, *outs, token_ref, bank, column, coh, spec, xs, norms, out_ref, bank_sems, out_sem = refs[count:]
    half = PEERS * CAP
    loads = [pltpu.make_async_copy(banks[i], bank.at[i], bank_sems.at[i]) for i in range(count)]
    for load in loads:
        load.start()
    table = jnp.concatenate([packet_ref[s, :, 2 * WIDE : 2 * WIDE + 128] for s in range(PEERS)], 0)
    column[...] = jnp.transpose(table)
    for s in range(PEERS):
        for p in range(2):
            coh[2 * s + p : 2 * s + p + 1, :] = packet_ref[s, :, p * WIDE : (p + 1) * WIDE]
    lane = lax.broadcasted_iota(jnp.int32, (CAP, SLOTS), 1).astype(jnp.float32)

    def block(i, _):
        for j in range(count):

            @pl.when(i == j)
            def _(j=j):
                loads[j].wait()

        want = column[pl.ds(pl.multiple_of(first + i * CAP, CAP), CAP), :]
        hot = jnp.concatenate(
            [(want[:, s : s + 1] == lane).astype(jnp.float32) for s in range(PEERS)], 0
        ).astype(jnp.bfloat16)
        for f2 in range(CLASSES):
            at = f2 * 256
            xs[f2, :half, :256] = jnp.dot(
                hot, bank[i, :, at : at + 256], preferred_element_type=jnp.float32
            )
        square = jnp.zeros((half, 128), jnp.float32)
        for f2 in range(CLASSES):
            at = f2 * 256
            tr, ti = xs[f2, :half, :128], xs[f2, :half, 128:256]
            square = square + (tr * tr + ti * ti)
            for s in range(PEERS):
                rs = slice(s * CAP, (s + 1) * CAP)
                trs, tis = tr[rs], ti[rs]
                for p in range(2):
                    nr = coh[2 * s + p : 2 * s + p + 1, at : at + 128]
                    ni = coh[2 * s + p : 2 * s + p + 1, at + 128 : at + 256]
                    to = slice(p * half + s * CAP, p * half + (s + 1) * CAP)
                    spec[f2, to, 0:128] = (nr * trs + ni * tis).astype(jnp.bfloat16)
                    spec[f2, to, 128:256] = (ni * trs - nr * tis).astype(jnp.bfloat16)
        norms[...] = jnp.broadcast_to(jnp.sum(square, axis=1, keepdims=True), (half, 128))

        for f2 in range(CLASSES):
            xs[f2] = jnp.dot(spec[f2], basis_ref[f2], preferred_element_type=jnp.float32)

        def tile(s, _):
            row = pl.multiple_of(s * CAP, CAP)
            norm = norms[pl.ds(row, CAP), :]
            good = norm > 0.0
            scale = jnp.where(good, 1.0 / jnp.where(good, norm, 1.0), 0.0)
            offset = jnp.where(good, 0.0, -1.0)
            for h in range(T1 // 128):
                parts = [[] for _ in range(QS)]
                for u in range(CAP // 8):
                    power = [None] * QS
                    for p in range(2):
                        rows = pl.ds(p * half + row + 8 * u, 8)

                        def load(f2, rows=rows, h=h):
                            return (
                                xs[f2, rows, h * 128 : (h + 1) * 128],
                                xs[f2, rows, T1 + h * 128 : T1 + (h + 1) * 128],
                            )

                        for q, (re, im) in enumerate(lags_of(load)):
                            w = re * re + im * im
                            power[q] = w if p == 0 else power[q] + w
                    for q in range(QS):
                        v = power[q] * scale[8 * u : 8 * u + 8] + offset[8 * u : 8 * u + 8]
                        parts[q].append(jnp.minimum(v, BIG))
                for q in range(QS):
                    v = jnp.concatenate(parts[q], 0).astype(jnp.bfloat16)
                    out_ref[s, i, :, q * T1 + h * 128 : q * T1 + (h + 1) * 128] = v
            return 0

        lax.fori_loop(0, PEERS, tile, 0, unroll=4)
        return 0

    lax.fori_loop(0, count, block, 0)
    if spread:
        x, c = lax.axis_index("seg") // (NZ * NC), lax.axis_index("seg") % NC
        puts = [
            pltpu.make_async_copy(
                out_ref.at[((x + dx) % NX) * NC + (c + dc) % NC], outs[dx * NC + dc], out_sem.at[dx * NC + dc]
            )
            for dx in range(NX)
            for dc in range(NC)
        ]
    else:
        puts = [pltpu.make_async_copy(out_ref, outs[0].at[:, pl.ds(slot, count)], out_sem.at[0])]
    for put in puts:
        put.start()
    token_ref[...] = norms[0:8, :]
    for put in puts:
        put.wait()


def filter_banks(banks, first, packet, basis, slot, total, before, spread=False):
    count = len(banks)
    vmem = pl.BlockSpec(memory_space=pltpu.VMEM)
    any_space = pl.BlockSpec(memory_space=pl.ANY)
    half = PEERS * CAP
    return pl.pallas_call(
        functools.partial(filter_kernel, count, first, slot, spread),
        out_shape=[
            jax.ShapeDtypeStruct(shape, jnp.bfloat16)
            for shape in ([(count, CAP, STEP)] * PEERS if spread else [(PEERS, total, CAP, STEP)])
        ]
        + [jax.ShapeDtypeStruct((8, 128), jnp.float32)],
        in_specs=[any_space] * count + [vmem, vmem, any_space],
        out_specs=[any_space] * (PEERS if spread else 1) + [vmem],
        input_output_aliases={count + 2: 0} if slot else {},
        scratch_shapes=[
            pltpu.VMEM((count, SLOTS, WIDE), jnp.bfloat16),
            pltpu.VMEM((128, PEERS), jnp.float32),
            pltpu.VMEM((2 * PEERS, WIDE), jnp.float32),
            pltpu.VMEM((CLASSES, 2 * half, 256), jnp.bfloat16),
            pltpu.VMEM((CLASSES, 2 * half, 2 * T1), jnp.float32),
            pltpu.VMEM((half, 128), jnp.float32),
            pltpu.VMEM((PEERS, count, CAP, STEP), jnp.bfloat16),
            pltpu.SemaphoreType.DMA((count,)),
            pltpu.SemaphoreType.DMA((PEERS,)),
        ],
        compiler_params=pltpu.CompilerParams(vmem_limit_bytes=24 << 20),
        cost_estimate=pl.CostEstimate(
            flops=0 if spread else count * (3 << 30), bytes_accessed=1 << 20, transcendentals=0
        ),
        name=f"filter{count}_{first}",
    )(*banks, packet, basis, before)


def order_kernel(near_ref, *refs):
    *pieces, place_ref, out_ref, far = refs
    count = pieces[0].shape[0]
    x, c = lax.axis_index("seg") // (NZ * NC), lax.axis_index("seg") % NC

    @pl.when(pl.program_id(0) == 0)
    def _():
        for dx in range(NX):
            for dc in range(NC):
                peer = ((x + NX - dx) % NX) * NC + (c + dc) % NC
                rows = pl.ds(pl.multiple_of(peer * count, CAP), count)
                far[rows, :] = pieces[dx * NC + dc][...]

    column = jnp.transpose(place_ref[...])[:, 0:1]
    out, first = None, 0
    for ref in (near_ref, far):
        n = ref.shape[0]
        lane = (first + lax.broadcasted_iota(jnp.int32, (column.shape[0], n), 1)).astype(jnp.float32)
        pick = (column == lane).astype(jnp.bfloat16)
        part = jnp.dot(pick, ref[...], preferred_element_type=jnp.float32)
        out = part if out is None else out + part
        first += n
    out_ref[...] = jnp.where(out < 0.0, jnp.nan, out)


def order_rows(near, pieces, place):
    n = place.shape[1]
    step = 256
    whole = [pl.BlockSpec(r.shape, lambda i: (0, 0)) for r in [near, *pieces]]
    return pl.pallas_call(
        order_kernel,
        out_shape=jax.ShapeDtypeStruct((n, STEP), jnp.float32),
        grid=(n // step,),
        in_specs=whole + [pl.BlockSpec((8, step), lambda i: (0, i))],
        out_specs=pl.BlockSpec((step, STEP), lambda i: (i, 0)),
        scratch_shapes=[pltpu.VMEM((PEERS * pieces[0].shape[0], STEP), jnp.bfloat16)],
        compiler_params=pltpu.CompilerParams(vmem_limit_bytes=24 << 20),
        cost_estimate=pl.CostEstimate(flops=1 << 30, bytes_accessed=4 << 20, transcendentals=0),
        name="order_rows",
    )(near, *pieces, place)


def per_device(basis, strain, antenna, delays, template_bank, duration_bin, owner_seg, slot_index):
    def at(x, z, c):
        return (x * NZ + z) * NC + c

    places = [(x, z, c) for x in range(NX) for z in range(NZ) for c in range(NC)]
    groups = [[at(x, z, c) for x in range(NX) for c in range(NC)] for z in range(NZ)]
    up = [(at(x, z, c), at(x, (z + 1) % NZ, c)) for x, z, c in places]
    down = [(at(x, z, c), at(x, (z - 1) % NZ, c)) for x, z, c in places]
    groups = [[i * ND + d for i in group for d in range(ND)] for group in groups]
    back_groups = [[at(x, z, c) for x in range(NX) for c in range(NC)] for z in range(NZ)]
    half = SLOTS // 2

    with jax.named_scope("head"):
        own, packet, place = head(
            duration_bin,
            delays,
            template_bank[0],
            strain.reshape(WIDE // 128, 128),
            owner_seg.reshape(1, -1),
            slot_index,
        )

    held = {0: own}

    def ring(k):
        with jax.named_scope("ring"):
            if k < 4:
                held[-k] = lax.ppermute(held[1 - k], "seg", up)
                held[k] = lax.ppermute(held[k - 1], "seg", down)
            else:
                held[4] = jnp.concatenate(
                    [lax.ppermute(held[-3][:half], "seg", up), lax.ppermute(held[3][half:], "seg", down)], 0
                )

    ring(1)
    with jax.named_scope("exchange"):
        packet = lax.all_to_all(
            packet, ("seg", "det"), split_axis=0, concat_axis=0, tiled=True, axis_index_groups=groups
        )
        packet, held[1], held[-1] = lax.optimization_barrier((packet, held[1], held[-1]))
        packet = combine(antenna, packet)
    ring(2)

    near_part, far_part = PARTS
    rows, slot, token = place, 0, place
    for step in CALLS[near_part]:
        with jax.named_scope("filter"):
            rows, token = filter_banks(
                [held[d] for d in step], slot * CAP, packet, basis, slot, len(near_part), rows
            )
        slot += len(step)
        k = max(held)
        token, held[k], held[-k] = lax.optimization_barrier((token, held[k], held[-k]))
        ring(k + 1)
    with jax.named_scope("back"):
        near = lax.all_to_all(
            rows.reshape(PEERS, slot * CAP, STEP),
            "seg",
            split_axis=0,
            concat_axis=0,
            tiled=True,
            axis_index_groups=back_groups,
        )
    m = len(far_part)
    token, late_basis = lax.optimization_barrier((token, basis))
    late_basis = stage(late_basis)
    with jax.named_scope("filter"):
        *pieces, token = filter_banks(
            [held[d] for d in far_part], slot * CAP, packet, late_basis, 0, m, token, spread=True
        )
    with jax.named_scope("back"):
        for k in range(1, PEERS):
            dx, dc = divmod(k, NC)
            to = [(at(x, z, c), at((x + dx) % NX, z, (c + dc) % NC)) for x, z, c in places]
            pieces[k] = lax.ppermute(pieces[k], "seg", to)
    with jax.named_scope("order"):
        near = near.reshape(PEERS * slot * CAP, STEP)
        return order_rows(near, [p.reshape(m * CAP, STEP) for p in pieces], place)[None]


def solution(mesh):
    basis = class_basis()
    in_specs = (
        P("det", "seg", None),
        P(),
        P(),
        P("seg", "det", None),
        P("seg", "det"),
        P("seg", "det", None),
        P("seg", "det"),
    )

    def run(*args):
        return jax.shard_map(
            lambda *a: per_device(jnp.asarray(basis), *a),
            mesh=mesh,
            in_specs=in_specs,
            out_specs=P("seg", "det", None),
            check_vma=False,
        )(*args)

    return run
```

```python
import functools
import math

import jax
import jax.numpy as jnp
import numpy as np
from jax import lax
from jax.experimental import pallas as pl
from jax.experimental.pallas import tpu as pltpu
from jax.sharding import PartitionSpec as P

HALF = 2048
WIDE = 2 * HALF
STEP = 1024
NX, NZ, NC = 4, 8, 2
PEERS = NX * NC
ND = 4
CAP = 16
SLOTS = 64
CLASSES = 16
T1 = 256
QS = 4
BIG = 3.0e38
CALLS = {(0, -1, 1, -2, 2): ((0, -1, 1), (-2, 2)), (-3, 3, 4): ((-3, 3), (4,))}
PARTS = tuple(CALLS)

LANE = np.arange(128)
FREQ = 128 * (LANE % 16)[None, :] + 16 * (LANE // 16)[None, :] + np.arange(CLASSES)[:, None]


def class_basis():
    t = np.arange(T1)
    ang = ((FREQ[:, :, None] * t[None, None, :]) % WIDE) * (math.pi / HALF)
    c, s = np.cos(ang), np.sin(ang)
    upper = np.concatenate([c, s], 2)
    lower = np.concatenate([-s, c], 2)
    return np.concatenate([upper, lower], 1).astype(np.float32).astype(jnp.bfloat16)


def to_classes(x, lane):
    for k in range(4):
        b = 1 << k
        up = (lane & b) != 0
        for g in range(16):
            if g & b:
                continue
            lo, hi = x[g], x[g | b]
            x[g] = jnp.where(up, pltpu.roll(hi, b, 1), lo)
            x[g | b] = jnp.where(up, hi, pltpu.roll(lo, 128 - b, 1))
    return x


def lookup(dz, values):
    out = jnp.zeros_like(dz)
    for d, v in enumerate(values):
        if v:
            out = jnp.where(dz == d, v, out)
    return out


def head_kernel(
    dur_ref, delays_ref, bank_ref, strain_ref, owner_ref, slot_ref, own_ref, packet_ref, place_ref
):
    det, my_z = lax.axis_index("det"), (lax.axis_index("seg") // NC) % NZ
    owner = owner_ref[...]
    n = owner.shape[1]
    peer = (owner // (NZ * NC)) * NC + (owner & 1)
    dz = ((owner >> 1) - my_z) & (NZ - 1)
    part_of, order_of, first_of = [0] * NZ, [0] * NZ, [0] * NZ
    first = 0
    for g, part in enumerate(PARTS):
        for j, d in enumerate(part):
            part_of[d % NZ], order_of[d % NZ], first_of[d % NZ] = g, j, first
        first += len(part) * CAP
    hot = owner == lax.broadcasted_iota(jnp.int32, (PEERS * NZ, n), 0)
    earlier = lax.broadcasted_iota(jnp.int32, (n, n), 0) < lax.broadcasted_iota(jnp.int32, (n, n), 1)
    before = jnp.dot(
        hot.astype(jnp.float32).astype(jnp.bfloat16),
        earlier.astype(jnp.float32).astype(jnp.bfloat16),
        preferred_element_type=jnp.float32,
    )
    rank = jnp.sum(jnp.where(hot, before, 0.0), axis=0, keepdims=True).astype(jnp.int32)
    start = lookup(dz, first_of)
    rank = rank + CAP * lookup(dz, order_of)
    want = (slot_ref[...] + 1).astype(jnp.float32)
    size = lookup(dz, [len(PARTS[g]) * CAP for g in part_of])
    place = (start * PEERS + peer * size + rank).astype(jnp.float32)
    place_ref[...] = jnp.broadcast_to(place, (8, n))
    wanted = jnp.where(peer == lax.broadcasted_iota(jnp.int32, (PEERS, n), 0), want, 0.0)
    spot = (start + rank) == lax.broadcasted_iota(jnp.int32, (NZ * CAP, n), 0)
    table = (
        lax.dot_general(
            wanted.astype(jnp.bfloat16),
            spot.astype(jnp.float32).astype(jnp.bfloat16),
            (((1,), (1,)), ((), ())),
            preferred_element_type=jnp.float32,
        )
        - 1.0
    )

    delay = delays_ref[det]
    row16 = lax.broadcasted_iota(jnp.int32, (16, 128), 0)
    lane16 = lax.broadcasted_iota(jnp.int32, (16, 128), 1)
    freq = row16 * 128 + lane16
    phase = ((freq * delay) & (WIDE - 1)).astype(jnp.float32) * (-math.pi / HALF)
    cos_rot, sin_rot = jnp.cos(phase), jnp.sin(phase)
    re, im = strain_ref[0:16, :], strain_ref[16:32, :]
    lane1 = lax.broadcasted_iota(jnp.int32, (1, 128), 1)
    for c, x in enumerate((re * cos_rot - im * sin_rot, re * sin_rot + im * cos_rot)):
        x = to_classes([x[g : g + 1, :] for g in range(16)], lane1)
        for f2 in range(CLASSES):
            at = f2 * 256 + c * 128
            packet_ref[0, :, at : at + 128] = x[f2]
    shifted = packet_ref[0, :, 0:WIDE]
    for m in range(PEERS * ND):
        if m:
            packet_ref[m, :, 0:WIDE] = shifted
        packet_ref[m, :, WIDE:] = table[m // ND : m // ND + 1, :]

    def rows(i, _):
        r = pl.ds(pl.multiple_of(i * 16, 16), 16)
        dur = jnp.zeros((16, 128), jnp.int32)
        for j in range(16):
            dur = jnp.where(row16 == j, dur_ref[0, i * 16 + j], dur)
        for c in range(2):
            x = []
            for g in range(16):
                v = bank_ref[r, c * HALF + g * 128 : c * HALF + (g + 1) * 128].astype(jnp.float32)
                x.append(jnp.where(dur <= g, v, 0.0))
            x = to_classes(x, lane16)
            for f2 in range(CLASSES):
                at = f2 * 256 + c * 128
                own_ref[r, at : at + 128] = x[f2].astype(jnp.bfloat16)
        return 0

    lax.fori_loop(0, SLOTS // 16, rows, 0)


def head(dur, delays, bank, strain, owner, slot):
    n = owner.shape[1]
    vmem = pl.BlockSpec(memory_space=pltpu.VMEM)
    smem = pl.BlockSpec(memory_space=pltpu.SMEM)
    return pl.pallas_call(
        head_kernel,
        out_shape=[
            jax.ShapeDtypeStruct((SLOTS, WIDE), jnp.bfloat16),
            jax.ShapeDtypeStruct((PEERS * ND, 1, WIDE + 128), jnp.float32),
            jax.ShapeDtypeStruct((8, n), jnp.float32),
        ],
        in_specs=[smem] * 2 + [vmem] * 4,
        out_specs=[vmem] * 3,
        compiler_params=pltpu.CompilerParams(vmem_limit_bytes=58 << 20),
        cost_estimate=pl.CostEstimate(flops=8 << 30, bytes_accessed=2 << 20, transcendentals=0),
        name="head",
    )(dur, delays, bank, strain, owner, slot)


def combine_kernel(antenna_ref, packet_ref, out_ref):
    det = lax.axis_index("det")
    for s in range(PEERS):
        rows = [packet_ref[s * ND + d, :, 0:WIDE] for d in range(ND)]
        for p in range(2):
            total = antenna_ref[p, 0] * rows[0]
            for d in range(1, ND):
                total = total + antenna_ref[p, d] * rows[d]
            out_ref[s, :, p * WIDE : (p + 1) * WIDE] = total
        out_ref[s, :, 2 * WIDE :] = packet_ref[s * ND + det, :, WIDE:]


def combine(antenna, packet):
    vmem = pl.BlockSpec(memory_space=pltpu.VMEM)
    smem = pl.BlockSpec(memory_space=pltpu.SMEM)
    return pl.pallas_call(
        combine_kernel,
        out_shape=jax.ShapeDtypeStruct((PEERS, 1, 2 * WIDE + 128), jnp.float32),
        in_specs=[smem, vmem],
        out_specs=vmem,
        compiler_params=pltpu.CompilerParams(vmem_limit_bytes=16 << 20),
        cost_estimate=pl.CostEstimate(flops=4 << 30, bytes_accessed=1 << 20, transcendentals=0),
        name="combine",
    )(antenna, packet)


def rotate(re, im, k):
    k %= 16
    if k == 0:
        return re, im
    if k == 4:
        return -im, re
    if k == 8:
        return -re, -im
    if k == 12:
        return im, -re
    r = math.sqrt(0.5)
    if k == 2:
        return (re - im) * r, (re + im) * r
    if k == 6:
        return (re + im) * -r, (re - im) * r
    c, s = math.cos(math.pi * k / 8), math.sin(math.pi * k / 8)
    return re * c - im * s, re * s + im * c


def cadd(a, b):
    return a[0] + b[0], a[1] + b[1]


def csub(a, b):
    return a[0] - b[0], a[1] - b[1]


def lags_of(load):
    def four(a):
        x0, x1, x2, x3 = load(a), load(a + 4), load(a + 8), load(a + 12)
        e0, e1, o0, o1 = cadd(x0, x2), csub(x0, x2), cadd(x1, x3), csub(x1, x3)
        turned = (-o1[1], o1[0])
        return [cadd(e0, o0), cadd(e1, turned), csub(e0, o0), csub(e1, turned)]

    def pair(a):
        y, z = four(a), four(a + 2)
        return [cadd(y[q], rotate(*z[q], 2 * q)) for q in range(QS)]

    even, odd = pair(0), pair(1)
    return [cadd(even[q], rotate(*odd[q], q)) for q in range(QS)]


def stage_kernel(source, out_ref, sem):
    copy = pltpu.make_async_copy(source, out_ref, sem)
    copy.start()
    copy.wait()


def stage(basis):
    return pl.pallas_call(
        stage_kernel,
        out_shape=jax.ShapeDtypeStruct(basis.shape, basis.dtype),
        in_specs=[pl.BlockSpec(memory_space=pl.ANY)],
        out_specs=pl.BlockSpec(memory_space=pltpu.VMEM),
        scratch_shapes=[pltpu.SemaphoreType.DMA],
        compiler_params=pltpu.CompilerParams(vmem_limit_bytes=16 << 20),
        cost_estimate=pl.CostEstimate(flops=0, bytes_accessed=8 << 20, transcendentals=0),
        name="stage_basis",
    )(basis)


def filter_kernel(count, first, slot, spread, *refs):
    banks = refs[:count]
    packet_ref, basis_ref, *outs, token_ref, bank, column, coh, spec, xs, norms, out_ref, bank_sems, out_sem = refs[count:]
    half = PEERS * CAP
    loads = [pltpu.make_async_copy(banks[i], bank.at[i], bank_sems.at[i]) for i in range(count)]
    for load in loads:
        load.start()
    table = jnp.concatenate([packet_ref[s, :, 2 * WIDE : 2 * WIDE + 128] for s in range(PEERS)], 0)
    column[...] = jnp.transpose(table)
    for s in range(PEERS):
        for p in range(2):
            coh[2 * s + p : 2 * s + p + 1, :] = packet_ref[s, :, p * WIDE : (p + 1) * WIDE]
    lane = lax.broadcasted_iota(jnp.int32, (CAP, SLOTS), 1).astype(jnp.float32)

    def block(i, _):
        for j in range(count):

            @pl.when(i == j)
            def _(j=j):
                loads[j].wait()

        want = column[pl.ds(pl.multiple_of(first + i * CAP, CAP), CAP), :]
        hot = jnp.concatenate(
            [(want[:, s : s + 1] == lane).astype(jnp.float32) for s in range(PEERS)], 0
        ).astype(jnp.bfloat16)
        for f2 in range(CLASSES):
            at = f2 * 256
            xs[f2, :half, :256] = jnp.dot(
                hot, bank[i, :, at : at + 256], preferred_element_type=jnp.float32
            )
        square = jnp.zeros((half, 128), jnp.float32)
        for f2 in range(CLASSES):
            at = f2 * 256
            tr, ti = xs[f2, :half, :128], xs[f2, :half, 128:256]
            square = square + (tr * tr + ti * ti)
            for s in range(PEERS):
                rs = slice(s * CAP, (s + 1) * CAP)
                trs, tis = tr[rs], ti[rs]
                for p in range(2):
                    nr = coh[2 * s + p : 2 * s + p + 1, at : at + 128]
                    ni = coh[2 * s + p : 2 * s + p + 1, at + 128 : at + 256]
                    to = slice(p * half + s * CAP, p * half + (s + 1) * CAP)
                    spec[f2, to, 0:128] = (nr * trs + ni * tis).astype(jnp.bfloat16)
                    spec[f2, to, 128:256] = (ni * trs - nr * tis).astype(jnp.bfloat16)
        norms[...] = jnp.broadcast_to(jnp.sum(square, axis=1, keepdims=True), (half, 128))

        for f2 in range(CLASSES):
            xs[f2] = jnp.dot(spec[f2], basis_ref[f2], preferred_element_type=jnp.float32)

        def tile(s, _):
            row = pl.multiple_of(s * CAP, CAP)
            norm = norms[pl.ds(row, CAP), :]
            good = norm > 0.0
            scale = jnp.where(good, 1.0 / jnp.where(good, norm, 1.0), 0.0)
            offset = jnp.where(good, 0.0, -1.0)
            for h in range(T1 // 128):
                parts = [[] for _ in range(QS)]
                for u in range(CAP // 8):
                    power = [None] * QS
                    for p in range(2):
                        rows = pl.ds(p * half + row + 8 * u, 8)

                        def load(f2, rows=rows, h=h):
                            return (
                                xs[f2, rows, h * 128 : (h + 1) * 128],
                                xs[f2, rows, T1 + h * 128 : T1 + (h + 1) * 128],
                            )

                        for q, (re, im) in enumerate(lags_of(load)):
                            w = re * re + im * im
                            power[q] = w if p == 0 else power[q] + w
                    for q in range(QS):
                        v = power[q] * scale[8 * u : 8 * u + 8] + offset[8 * u : 8 * u + 8]
                        parts[q].append(jnp.minimum(v, BIG))
                for q in range(QS):
                    v = jnp.concatenate(parts[q], 0).astype(jnp.bfloat16)
                    out_ref[s, i, :, q * T1 + h * 128 : q * T1 + (h + 1) * 128] = v
            return 0

        lax.fori_loop(0, PEERS, tile, 0, unroll=4)
        return 0

    lax.fori_loop(0, count, block, 0)
    outs = outs[len(outs) - (PEERS if spread else 1) :]
    if spread:
        x, c = lax.axis_index("seg") // (NZ * NC), lax.axis_index("seg") % NC
        puts = [
            pltpu.make_async_copy(
                out_ref.at[((x + dx) % NX) * NC + (c + dc) % NC],
                outs[dx * NC + dc].at[pl.ds(slot, count)],
                out_sem.at[dx * NC + dc],
            )
            for dx in range(NX)
            for dc in range(NC)
        ]
    else:
        puts = [pltpu.make_async_copy(out_ref, outs[0].at[:, pl.ds(slot, count)], out_sem.at[0])]
    for put in puts:
        put.start()
    token_ref[...] = norms[0:8, :]
    for put in puts:
        put.wait()


def filter_banks(banks, first, packet, basis, slot, total, before, spread=False):
    count = len(banks)
    vmem = pl.BlockSpec(memory_space=pltpu.VMEM)
    any_space = pl.BlockSpec(memory_space=pl.ANY)
    half = PEERS * CAP
    return pl.pallas_call(
        functools.partial(filter_kernel, count, first, slot, spread),
        out_shape=[
            jax.ShapeDtypeStruct(shape, jnp.bfloat16)
            for shape in ([(total, CAP, STEP)] * PEERS if spread else [(PEERS, total, CAP, STEP)])
        ]
        + [jax.ShapeDtypeStruct((8, 128), jnp.float32)],
        in_specs=[any_space] * count + [vmem, vmem] + [any_space] * len(before),
        out_specs=[any_space] * (PEERS if spread else 1) + [vmem],
        input_output_aliases={count + 2 + k: k for k in range(len(before))} if slot else {},
        scratch_shapes=[
            pltpu.VMEM((count, SLOTS, WIDE), jnp.bfloat16),
            pltpu.VMEM((128, PEERS), jnp.float32),
            pltpu.VMEM((2 * PEERS, WIDE), jnp.float32),
            pltpu.VMEM((CLASSES, 2 * half, 256), jnp.bfloat16),
            pltpu.VMEM((CLASSES, 2 * half, 2 * T1), jnp.float32),
            pltpu.VMEM((half, 128), jnp.float32),
            pltpu.VMEM((PEERS, count, CAP, STEP), jnp.bfloat16),
            pltpu.SemaphoreType.DMA((count,)),
            pltpu.SemaphoreType.DMA((PEERS,)),
        ],
        compiler_params=pltpu.CompilerParams(vmem_limit_bytes=24 << 20),
        cost_estimate=pl.CostEstimate(
            flops=0 if spread else count * (3 << 30), bytes_accessed=1 << 20, transcendentals=0
        ),
        name=f"filter{count}_{first}",
    )(*banks, packet, basis, *before)


def order_kernel(near_ref, *refs):
    *pieces, place_ref, out_ref, far = refs
    count = pieces[0].shape[0]
    x, c = lax.axis_index("seg") // (NZ * NC), lax.axis_index("seg") % NC

    @pl.when(pl.program_id(0) == 0)
    def _():
        for dx in range(NX):
            for dc in range(NC):
                peer = ((x + NX - dx) % NX) * NC + (c + dc) % NC
                rows = pl.ds(pl.multiple_of(peer * count, CAP), count)
                far[rows, :] = pieces[dx * NC + dc][...]

    column = jnp.transpose(place_ref[...])[:, 0:1]
    out, first = None, 0
    for ref in (near_ref, far):
        n = ref.shape[0]
        lane = (first + lax.broadcasted_iota(jnp.int32, (column.shape[0], n), 1)).astype(jnp.float32)
        pick = (column == lane).astype(jnp.bfloat16)
        part = jnp.dot(pick, ref[...], preferred_element_type=jnp.float32)
        out = part if out is None else out + part
        first += n
    out_ref[...] = jnp.where(out < 0.0, jnp.nan, out)


def order_rows(near, pieces, place):
    n = place.shape[1]
    step = 256
    whole = [pl.BlockSpec(r.shape, lambda i: (0, 0)) for r in [near, *pieces]]
    return pl.pallas_call(
        order_kernel,
        out_shape=jax.ShapeDtypeStruct((n, STEP), jnp.float32),
        grid=(n // step,),
        in_specs=whole + [pl.BlockSpec((8, step), lambda i: (0, i))],
        out_specs=pl.BlockSpec((step, STEP), lambda i: (i, 0)),
        scratch_shapes=[pltpu.VMEM((PEERS * pieces[0].shape[0], STEP), jnp.bfloat16)],
        compiler_params=pltpu.CompilerParams(vmem_limit_bytes=24 << 20),
        cost_estimate=pl.CostEstimate(flops=1 << 30, bytes_accessed=4 << 20, transcendentals=0),
        name="order_rows",
    )(near, *pieces, place)


def per_device(basis, strain, antenna, delays, template_bank, duration_bin, owner_seg, slot_index):
    def at(x, z, c):
        return (x * NZ + z) * NC + c

    places = [(x, z, c) for x in range(NX) for z in range(NZ) for c in range(NC)]
    groups = [[at(x, z, c) for x in range(NX) for c in range(NC)] for z in range(NZ)]
    up = [(at(x, z, c), at(x, (z + 1) % NZ, c)) for x, z, c in places]
    down = [(at(x, z, c), at(x, (z - 1) % NZ, c)) for x, z, c in places]
    groups = [[i * ND + d for i in group for d in range(ND)] for group in groups]
    back_groups = [[at(x, z, c) for x in range(NX) for c in range(NC)] for z in range(NZ)]
    half = SLOTS // 2

    with jax.named_scope("head"):
        own, packet, place = head(
            duration_bin,
            delays,
            template_bank[0],
            strain.reshape(WIDE // 128, 128),
            owner_seg.reshape(1, -1),
            slot_index,
        )

    held = {0: own}

    def ring(k):
        with jax.named_scope("ring"):
            if k < 4:
                held[-k] = lax.ppermute(held[1 - k], "seg", up)
                held[k] = lax.ppermute(held[k - 1], "seg", down)
            else:
                held[4] = jnp.concatenate(
                    [lax.ppermute(held[-3][:half], "seg", up), lax.ppermute(held[3][half:], "seg", down)], 0
                )

    ring(1)
    with jax.named_scope("exchange"):
        packet = lax.all_to_all(
            packet, ("seg", "det"), split_axis=0, concat_axis=0, tiled=True, axis_index_groups=groups
        )
        packet, held[1], held[-1] = lax.optimization_barrier((packet, held[1], held[-1]))
        packet = combine(antenna, packet)
    ring(2)

    near_part, far_part = PARTS
    rows, slot, token = [place], 0, place
    for step in CALLS[near_part]:
        with jax.named_scope("filter"):
            *rows, token = filter_banks(
                [held[d] for d in step], slot * CAP, packet, basis, slot, len(near_part), rows
            )
        slot += len(step)
        k = max(held)
        token, held[k], held[-k] = lax.optimization_barrier((token, held[k], held[-k]))
        ring(k + 1)
    with jax.named_scope("back"):
        near = lax.all_to_all(
            rows[0].reshape(PEERS, slot * CAP, STEP),
            "seg",
            split_axis=0,
            concat_axis=0,
            tiled=True,
            axis_index_groups=back_groups,
        )
    m = len(far_part)
    token, late_basis = lax.optimization_barrier((token, basis))
    late_basis = stage(late_basis)
    pieces, done = [token], 0
    for step in CALLS[far_part]:
        with jax.named_scope("filter"):
            *pieces, token = filter_banks(
                [held[d] for d in step],
                (slot + done) * CAP,
                packet,
                late_basis,
                done,
                m,
                pieces,
                spread=True,
            )
        done += len(step)
    with jax.named_scope("back"):
        for k in range(1, PEERS):
            dx, dc = divmod(k, NC)
            to = [(at(x, z, c), at((x + dx) % NX, z, (c + dc) % NC)) for x, z, c in places]
            pieces[k] = lax.ppermute(pieces[k], "seg", to)
    with jax.named_scope("order"):
        near = near.reshape(PEERS * slot * CAP, STEP)
        return order_rows(near, [p.reshape(m * CAP, STEP) for p in pieces], place)[None]


def solution(mesh):
    basis = class_basis()
    in_specs = (
        P("det", "seg", None),
        P(),
        P(),
        P("seg", "det", None),
        P("seg", "det"),
        P("seg", "det", None),
        P("seg", "det"),
    )

    def run(*args):
        return jax.shard_map(
            lambda *a: per_device(jnp.asarray(basis), *a),
            mesh=mesh,
            in_specs=in_specs,
            out_specs=P("seg", "det", None),
            check_vma=False,
        )(*args)

    return run
```
